512 devices in a mesh: dp: 32 (over x, z), expert: 16 (over y, core).
Axes of the slice: x: 4, y: 8, z: 8, core: 2. Of those that a mesh axis runs over, the one named last changes fastest.
Arguments:
- xin: bfloat16 [2, 4096, 8192], P(None, 'dp', 'expert'), may hold values from -6 to 6
- zin: bfloat16 [2, 4096, 8192], P(None, 'dp', 'expert'), may hold values from -6 to 6
- cotangent: bfloat16 [2, 4096, 8192], P(None, 'dp', 'expert'), may hold values from -6 to 6
- conv_weight: float32 [4, 8192], P(None, 'expert'), may hold values from -3 to 3
- conv_bias: float32 [8192], P('expert'), may hold values from -3 to 3
- proj_weight: bfloat16 [288, 8192], P('dp', 'expert'), may hold values from -0.0625 to 0.0625
- dt_weight: bfloat16 [256, 8192], P('dp', 'expert'), may hold values from -0.375 to 0.375
- dt_bias: float32 [8192], P('expert'), may hold values from -5 to -1
- a_log: float32 [16, 8192], P(None, 'expert'), may hold values from -8 to 2
- d_skip: float32 [8192], P('expert'), may hold values from 0.5 to 1.5
Outputs:
- grad_x: bfloat16 [2, 4096, 8192], P(None, 'dp', 'expert')
- grad_gate: bfloat16 [2, 4096, 8192], P(None, 'dp', 'expert')
- grad_proj_weight: float32 [256, 8192], P('dp', 'expert')
- grad_state_weight: float32 [32, 8192], P(None, 'expert')
- grad_dt_weight: float32 [256, 8192], P('dp', 'expert')
- grad_conv_weight: float32 [4, 8192], P(None, 'expert')
- grad_conv_bias: float32 [8192], P('expert')
- grad_dt_bias: float32 [8192], P('expert')
- grad_a_log: float32 [16, 8192], P(None, 'expert')
- grad_d_skip: float32 [8192], P('expert')
The draws below stay inside these ranges and needn't reach their ends.
All inputs are finite; a program needn't handle non-finite values.
Results may differ from the reference program's by a relative error of at most 0.007.
Values may be sent and summed in bfloat16 or wider, within the bound.
A program may use at most 64 MiB of HBM per device.

```python
import jax
import jax.numpy as jnp
from jax import lax

INNER = 8192
RANK = 256
STATE = 16
KERNEL = 4
BLOCK = 128
SEQS = 2
PROJ = 288
LEN = 4096


def level_of(rng, dims, cuts, smallest, top_value):
    def one(dim, shards_of):
        heights = jax.random.uniform(jax.random.fold_in(jax.random.fold_in(rng, 6), dim), (shards_of,), jnp.float32, smallest / len(cuts), top_value / len(cuts))
        return jnp.repeat(jnp.exp(heights), dims[dim] // shards_of).reshape((-1,) + (1,) * (len(dims) - dim - 1))

    gain = one(*cuts[0])
    for cut in cuts[1:]:
        gain = gain * one(*cut)
    return gain


def normal_values(stream_key, extent, width, reach, shards=(), dtype=jnp.bfloat16):
    factor_of = level_of(stream_key, extent, shards, -0.22, 0.18) if shards else 1.0
    drawn = jax.random.normal(stream_key, extent, jnp.float32) * width * factor_of
    return jnp.minimum(jnp.maximum(drawn, -reach), reach).astype(dtype)


def setup_inputs(seed: int = 0) -> dict:
    splits = jax.random.split(jax.random.key(seed), 11)
    xin = normal_values(splits[0], (SEQS, LEN, INNER), 1.0, 6.0, ((1, 32), (2, 16)))
    zin = normal_values(splits[1], (SEQS, LEN, INNER), 1.0, 6.0, ((1, 32), (2, 16)))
    cotangent = normal_values(splits[2], (SEQS, LEN, INNER), 1.0, 6.0, ((1, 32), (2, 16)))
    conv_weight = normal_values(splits[3], (KERNEL, INNER), KERNEL ** -0.5, 3.0, ((1, 16),), jnp.float32)
    conv_bias = normal_values(splits[4], (INNER,), 0.5, 3.0, ((0, 16),), jnp.float32)
    proj_weight = normal_values(splits[5], (PROJ, INNER), INNER ** -0.5, 0.0625, ((0, 32), (1, 16)))
    dt_weight = normal_values(splits[6], (RANK, INNER), RANK ** -0.5, 0.375, ((0, 32), (1, 16)))
    dt_bias = jnp.clip(-5.0 + 4.0 * jax.random.uniform(splits[7], (INNER,), jnp.float32) ** level_of(splits[7], (INNER,), ((0, 16),), -0.2, 0.2), -5.0, -1.0)
    a_log = jnp.clip(-8.0 + 10.0 * jax.random.uniform(splits[8], (STATE, INNER), jnp.float32) ** level_of(splits[8], (STATE, INNER), ((1, 16),), -0.2, 0.2), -8.0, 2.0)
    d_skip = jnp.clip(0.5 + 1.0 * jax.random.uniform(splits[9], (INNER,), jnp.float32) ** level_of(splits[9], (INNER,), ((0, 16),), -0.2, 0.2), 0.5, 1.5)
    return {"xin": xin, "zin": zin, "cotangent": cotangent, "conv_weight": conv_weight, "conv_bias": conv_bias, "proj_weight": proj_weight, "dt_weight": dt_weight, "dt_bias": dt_bias, "a_log": a_log, "d_skip": d_skip}


def scan_step(decay_rate, carried, step_now, x_now, b_now):
    decay_now = jnp.exp(step_now[None, :] * decay_rate)
    return decay_now * carried + b_now[:, None] * (step_now * x_now)[None, :]


def sequence_grads(x_seq, z_seq, g_seq, conv_weight, conv_bias, proj_weight, dt_weight, dt_bias, a_log, d_skip):
    kernel_len = conv_weight.shape[0]
    seq_len = x_seq.shape[0]
    x_input = x_seq.astype(jnp.float32)
    padded = jnp.concatenate([jnp.zeros((kernel_len - 1, x_input.shape[1]), jnp.float32), x_input], 0)
    preact = conv_bias[None, :] + jnp.zeros_like(x_input)
    for tap_index in range(kernel_len):
        preact = preact + conv_weight[tap_index][None, :] * padded[tap_index:tap_index + seq_len]
    pre_sig = jax.nn.sigmoid(preact)
    x_conv = (preact * pre_sig).astype(jnp.bfloat16)
    x_value = x_conv.astype(jnp.float32)
    projected = jnp.dot(x_conv, proj_weight.T, preferred_element_type=jnp.float32)
    dt_low = projected[:, :RANK].astype(jnp.bfloat16)
    b_matrix = projected[:, RANK:RANK + STATE]
    c_matrix = projected[:, RANK + STATE:]
    dt_pre = jnp.dot(dt_low, dt_weight, preferred_element_type=jnp.float32) + dt_bias[None, :]
    step_size = jax.nn.softplus(dt_pre)
    decay_rate = -jnp.exp(a_log)
    block_count = seq_len // BLOCK

    def by_block(values):
        return values.reshape((block_count, BLOCK) + values.shape[1:])

    def forward_block(carried, inputs):
        def single(inner, pieces):
            inner = scan_step(decay_rate, inner, pieces[0], pieces[1], pieces[2])
            return inner, jnp.sum(pieces[3][:, None] * inner, axis=0)
        carried_end, outputs = lax.scan(single, carried, inputs)
        return carried_end, (carried, outputs)

    zero_state = jnp.zeros(decay_rate.shape, jnp.float32)
    blocked = (by_block(step_size), by_block(x_value), by_block(b_matrix), by_block(c_matrix))
    unused, (starts, scan_out) = lax.scan(forward_block, zero_state, blocked)
    y_value = scan_out.reshape(seq_len, -1) + d_skip[None, :] * x_value

    z_value = z_seq.astype(jnp.float32)
    g_value = g_seq.astype(jnp.float32)
    z_sig = jax.nn.sigmoid(z_value)
    grad_gate = (g_value * y_value * z_sig * (1.0 + z_value * (1.0 - z_sig))).astype(jnp.bfloat16)
    grad_y = g_value * z_value * z_sig

    def backward_block(carried_in, inputs):
        begin_state, step_blk, x_blk, b_blk, c_blk, gy_blk = inputs

        def replay(inner, pieces):
            inner = scan_step(decay_rate, inner, pieces[0], pieces[1], pieces[2])
            return inner, inner

        unused_end, history = lax.scan(replay, begin_state, (step_blk, x_blk, b_blk))
        previous = jnp.concatenate([begin_state[None], history[:-1]], 0)

        def reverse_step(carried_now, pieces):
            passed, decay_grad = carried_now
            step_now, x_now, b_now, c_now, gy_now, state_now, state_prev = pieces
            decay_now = jnp.exp(step_now[None, :] * decay_rate)
            adjoint = c_now[:, None] * gy_now[None, :] + passed
            grad_c = jnp.sum(gy_now[None, :] * state_now, axis=1)
            grad_b = jnp.sum(adjoint * (step_now * x_now)[None, :], axis=1)
            b_adjoint = jnp.sum(b_now[:, None] * adjoint, axis=0)
            prev_term = adjoint * state_prev * decay_now
            grad_step = x_now * b_adjoint + jnp.sum(prev_term * decay_rate, axis=0)
            decay_grad = decay_grad + prev_term * step_now[None, :]
            return (decay_now * adjoint, decay_grad), (grad_c, grad_b, step_now * b_adjoint, grad_step)

        return lax.scan(reverse_step, carried_in, (step_blk, x_blk, b_blk, c_blk, gy_blk, history, previous), reverse=True)

    inputs_back = (starts, by_block(step_size), by_block(x_value), by_block(b_matrix), by_block(c_matrix), by_block(grad_y))
    (unused_pass, decay_total), outputs = lax.scan(backward_block, (zero_state, zero_state), inputs_back, reverse=True)
    grad_c, grad_b, grad_scan_x, grad_step = [member.reshape(seq_len, -1) for member in outputs]
    grad_dt_pre = grad_step * jax.nn.sigmoid(dt_pre)
    grad_dt_round = grad_dt_pre.astype(jnp.bfloat16)
    grad_low = jnp.dot(grad_dt_round, dt_weight.T, preferred_element_type=jnp.float32)
    grad_projected = jnp.concatenate([grad_low, grad_b, grad_c], 1).astype(jnp.bfloat16)
    grad_proj_weight = jnp.dot(grad_projected.T, x_conv, preferred_element_type=jnp.float32)
    grad_dt_weight = jnp.dot(dt_low.T, grad_dt_round, preferred_element_type=jnp.float32)
    grad_conv_x = d_skip[None, :] * grad_y + grad_scan_x + jnp.dot(grad_projected, proj_weight, preferred_element_type=jnp.float32)
    grad_preact = grad_conv_x * pre_sig * (1.0 + preact * (1.0 - pre_sig))
    grad_padded = jnp.concatenate([grad_preact, jnp.zeros((kernel_len - 1, grad_preact.shape[1]), jnp.float32)], 0)
    grad_input = jnp.zeros_like(grad_preact)
    for tap_index in range(kernel_len):
        shift_by = kernel_len - 1 - tap_index
        grad_input = grad_input + conv_weight[tap_index][None, :] * grad_padded[shift_by:shift_by + seq_len]
    grad_conv_weight = jnp.stack([jnp.sum(grad_preact * padded[tap_index:tap_index + seq_len], axis=0) for tap_index in range(kernel_len)], 0)
    return (grad_input.astype(jnp.bfloat16), grad_gate, grad_proj_weight, grad_dt_weight, grad_conv_weight,
            jnp.sum(grad_preact, axis=0), jnp.sum(grad_dt_pre, axis=0), decay_total, jnp.sum(grad_y * x_value, axis=0))


def reference(xin, zin, cotangent, conv_weight, conv_bias, proj_weight, dt_weight, dt_bias, a_log, d_skip):
    def per_sequence(pieces):
        return sequence_grads(pieces[0], pieces[1], pieces[2], conv_weight, conv_bias, proj_weight, dt_weight, dt_bias, a_log, d_skip)

    results = lax.map(per_sequence, (xin, zin, cotangent))
    totals = [jnp.sum(member, axis=0) for member in results[2:]]
    grad_a_log = totals[5] * (-jnp.exp(a_log))
    grad_full = totals[0]
    return (results[0], results[1], grad_full[:RANK], grad_full[RANK:], totals[1], totals[2], totals[3], totals[4], grad_a_log, totals[6])
```

```python
import functools

import jax
import jax.numpy as jnp
import numpy as np
from jax import lax
from jax.experimental import pallas as pl
from jax.experimental.pallas import tpu as pltpu
from jax.sharding import PartitionSpec as P

F32 = jnp.float32
BF16 = jnp.bfloat16
MESH = pl.DeviceIdType.MESH
LANES = 128
CHUNK = 16
VMEM_BYTES = 56 * 1024 * 1024

whole = pl.BlockSpec(memory_space=pltpu.VMEM)
sds = jax.ShapeDtypeStruct


def dot_nn(left, right, precision=None):
    return lax.dot_general(
        left, right, (((1,), (0,)), ((), ())), preferred_element_type=F32, precision=precision
    )


def dot_nt(left, right, precision=None):
    return lax.dot_general(
        left, right, (((1,), (1,)), ((), ())), preferred_element_type=F32, precision=precision
    )


def dot_tn(left, right):
    return lax.dot_general(left, right, (((0,), (0,)), ((), ())), preferred_element_type=F32)


def greet(axis, count):
    me = lax.axis_index(axis)
    barrier = pltpu.get_barrier_semaphore()

    def hail(k, carry):
        pl.semaphore_signal(
            barrier, inc=1, device_id={axis: lax.rem(me + k, count)}, device_id_type=MESH
        )
        return carry

    lax.fori_loop(1, count, hail, 0)
    pl.semaphore_wait(barrier, count - 1)
    return me


def send_all(axis, count, me, source, landing, send_sem, recv_sem):
    def one(k, carry):
        peer = lax.rem(me + k, count)
        pltpu.make_async_remote_copy(
            src_ref=source(peer),
            dst_ref=landing(me),
            send_sem=send_sem.at[k],
            recv_sem=recv_sem.at[k],
            device_id={axis: peer},
            device_id_type=MESH,
        ).start()
        return carry

    lax.fori_loop(1, count, one, 0)


def wait_all(axis, count, me, source, landing, send_sem, recv_sem, sent):
    def one(k, carry):
        peer = lax.rem(me + k, count)
        origin = lax.rem(me + count - k, count)
        copy = pltpu.make_async_remote_copy(
            src_ref=source(peer),
            dst_ref=landing(origin),
            send_sem=send_sem.at[k],
            recv_sem=recv_sem.at[k],
            device_id={axis: peer},
            device_id_type=MESH,
        )
        if sent:
            copy.wait_send()
        else:
            copy.wait_recv()
        return carry

    lax.fori_loop(1, count, one, 0)


class Exchange:
    def __init__(self, axis, count, me, source, landing, sems):
        self.args = (axis, count, me, source, landing, sems[0], sems[1])

    def start(self):
        send_all(*self.args)

    def wait_recv(self):
        wait_all(*self.args, False)

    def wait_send(self):
        wait_all(*self.args, True)


def pair_sems(count):
    return [pltpu.SemaphoreType.DMA((count,)), pltpu.SemaphoreType.DMA((count,))]


def comm_params(number):
    return pltpu.CompilerParams(
        collective_id=number, has_side_effects=True, vmem_limit_bytes=VMEM_BYTES
    )


def gather_body(count, block, extra, edge, block_all, extra_all, edge_in, s0, s1, s2, s3, s4, s5):
    me = greet("dp", count)
    halo = pltpu.make_async_remote_copy(
        src_ref=edge,
        dst_ref=edge_in,
        send_sem=s4,
        recv_sem=s5,
        device_id={"dp": lax.rem(me + 1, count)},
        device_id_type=MESH,
    )
    halo.start()
    first = Exchange("dp", count, me, lambda p: block, lambda d: block_all.at[d], (s0, s1))
    second = Exchange("dp", count, me, lambda p: extra, lambda d: extra_all.at[d], (s2, s3))
    first.start()
    second.start()
    block_all[me] = block[...]
    extra_all[me] = extra[...]
    halo.wait()
    first.wait_recv()
    second.wait_recv()
    first.wait_send()
    second.wait_send()


def gather_weights(block, extra, edge, count):
    return pl.pallas_call(
        functools.partial(gather_body, count),
        out_shape=(
            sds((count,) + block.shape, block.dtype),
            sds((count,) + extra.shape, extra.dtype),
            sds(edge.shape, edge.dtype),
        ),
        in_specs=[whole] * 3,
        out_specs=(whole,) * 3,
        scratch_shapes=pair_sems(count)
        + pair_sems(count)
        + [pltpu.SemaphoreType.DMA, pltpu.SemaphoreType.DMA],
        compiler_params=comm_params(1),
        name="gather_weights",
    )(block, extra, edge)


def reduce_body(count, low, bc, low_all, bc_all, low_slots, bc_slots, s0, s1, s2, s3, s4, s5, s6, s7):
    me = greet("expert", count)
    first = Exchange(
        "expert", count, me, lambda p: low.at[p], lambda d: low_slots.at[d], (s0, s1)
    )
    second = Exchange("expert", count, me, lambda p: bc.at[p], lambda d: bc_slots.at[d], (s2, s3))
    first.start()
    second.start()
    low_slots[me] = low[me]
    bc_slots[me] = bc[me]
    first.wait_recv()
    second.wait_recv()

    def add(k, total):
        return (total[0] + low_slots[k].astype(F32), total[1] + bc_slots[k])

    zero = (jnp.zeros(low.shape[1:], F32), jnp.zeros(bc.shape[1:], F32))
    low_sum, bc_sum = lax.fori_loop(0, count, add, zero)
    low_all[me] = low_sum.astype(BF16)
    bc_all[me] = bc_sum
    third = Exchange(
        "expert", count, me, lambda p: low_all.at[me], lambda d: low_all.at[d], (s4, s5)
    )
    fourth = Exchange(
        "expert", count, me, lambda p: bc_all.at[me], lambda d: bc_all.at[d], (s6, s7)
    )
    third.start()
    fourth.start()
    first.wait_send()
    second.wait_send()
    third.wait_recv()
    fourth.wait_recv()
    third.wait_send()
    fourth.wait_send()


def reduce_expert(low, bc, count, number):
    return pl.pallas_call(
        functools.partial(reduce_body, count),
        out_shape=(sds(low.shape, low.dtype), sds(bc.shape, bc.dtype)),
        in_specs=[whole] * 2,
        out_specs=(whole,) * 2,
        scratch_shapes=[pltpu.VMEM(low.shape, low.dtype), pltpu.VMEM(bc.shape, bc.dtype)]
        + pair_sems(count) * 4,
        compiler_params=comm_params(number),
        name="reduce_expert",
    )(low, bc)


def carry_body(count, parts, incoming, slots, found, s0, s1, s2, s3):
    me = greet("dp", count)
    first = Exchange("dp", count, me, lambda p: parts.at[p], lambda d: slots.at[d], (s0, s1))
    first.start()
    slots[me] = parts[me]
    first.wait_recv()

    def one(k, carried):
        ahead, behind = carried
        late = count - 1 - k
        found[k, 0:1, :] = ahead
        found[late, 1:2, :] = behind
        ahead = slots[k, 2:3, :] * ahead + slots[k, 0:1, :]
        behind = slots[late, 2:3, :] * behind + slots[late, 1:2, :]
        return (ahead, behind)

    zero = jnp.zeros((1, parts.shape[2]), F32)
    lax.fori_loop(0, count, one, (zero, zero))
    second = Exchange("dp", count, me, lambda p: found.at[p], lambda d: incoming.at[d], (s2, s3))
    second.start()
    incoming[me] = found[me]
    first.wait_send()
    second.wait_recv()
    second.wait_send()


def exchange_carries(parts, count):
    rows, width = parts.shape[0], parts.shape[2]
    return pl.pallas_call(
        functools.partial(carry_body, count),
        out_shape=sds((rows, 2, width), F32),
        in_specs=[whole],
        out_specs=whole,
        scratch_shapes=[pltpu.VMEM(parts.shape, F32), pltpu.VMEM((rows, 2, width), F32)]
        + pair_sems(count) * 2,
        compiler_params=comm_params(3),
        name="exchange_carries",
    )(parts)


def finish_body(
    count, big, small, edge, low_out, dt_out, small_all, edge_in, big_slots, small_slots,
    s0, s1, s2, s3, s4, s5, s6, s7,
):
    me = greet("dp", count)
    halo = pltpu.make_async_remote_copy(
        src_ref=edge,
        dst_ref=edge_in,
        send_sem=s6,
        recv_sem=s7,
        device_id={"dp": lax.rem(me + count - 1, count)},
        device_id_type=MESH,
    )
    halo.start()
    second = Exchange(
        "dp", count, me, lambda p: small.at[p], lambda d: small_slots.at[d], (s2, s3)
    )
    first = Exchange("dp", count, me, lambda p: big.at[p], lambda d: big_slots.at[d], (s0, s1))
    second.start()
    first.start()
    small_slots[me] = small[me]
    big_slots[me] = big[me]
    second.wait_recv()

    def add_small(k, total):
        return total + small_slots[k]

    small_all[me] = lax.fori_loop(0, count, add_small, jnp.zeros(small.shape[1:], F32))
    third = Exchange(
        "dp", count, me, lambda p: small_all.at[me], lambda d: small_all.at[d], (s4, s5)
    )
    third.start()
    first.wait_recv()

    def add_big(k, total):
        return total + big_slots[k].astype(F32)

    total = lax.fori_loop(0, count, add_big, jnp.zeros(big.shape[1:], F32))
    half = big.shape[1] // 2
    low_out[...] = total[:half]
    dt_out[...] = total[half:]
    halo.wait()
    third.wait_recv()
    second.wait_send()
    first.wait_send()
    third.wait_send()


def finish_sums(big, small, edge, count):
    half, width = big.shape[1] // 2, big.shape[2]
    return pl.pallas_call(
        functools.partial(finish_body, count),
        out_shape=(
            sds((half, width), F32),
            sds((half, width), F32),
            sds(small.shape, F32),
            sds(edge.shape, F32),
        ),
        in_specs=[whole] * 3,
        out_specs=(whole,) * 4,
        scratch_shapes=[pltpu.VMEM(big.shape, big.dtype), pltpu.VMEM(small.shape, F32)]
        + pair_sems(count) * 3
        + [pltpu.SemaphoreType.DMA, pltpu.SemaphoreType.DMA],
        compiler_params=comm_params(5),
        name="finish_sums",
    )(big, small, edge)


def local_call(body, outs, scratch, name, *args):
    return pl.pallas_call(
        body,
        out_shape=outs,
        in_specs=[whole] * len(args),
        out_specs=(whole,) * len(outs),
        scratch_shapes=scratch,
        compiler_params=pltpu.CompilerParams(vmem_limit_bytes=VMEM_BYTES),
        name=name,
    )(*args)


def conv_body(
    xin, front, block_all, extra_all, pick_dt, pick_low, pick_extra, weight, bias,
    preact_out, xconv_out, low_out, bc_out, proj_out, dt_out, padded, extra,
):
    seqs, tokens, width = xin.shape
    taps = weight.shape[0]
    devices = extra_all.shape[0]
    for i in range(devices):
        extra[i : i + 1, :] = extra_all[i]
    gathered = block_all[...].reshape(devices * block_all.shape[1], width)
    dt_out[...] = dot_nn(pick_dt[...], gathered).astype(BF16)
    proj = (
        dot_nn(pick_low[...], gathered) + dot_nn(pick_extra[...], extra[...].astype(BF16))
    ).astype(BF16)
    proj_out[...] = proj
    keep = jnp.where(lax.axis_index("dp") == 0, 0.0, 1.0).astype(F32)
    lead = front[...].astype(F32) * keep
    for s in range(seqs):
        padded[s, 8 - (taps - 1) : 8, :] = lead[s * (taps - 1) : (s + 1) * (taps - 1), :]
        padded[s, 8:, :] = xin[s].astype(F32)
        preact = bias[...] + jnp.zeros((tokens, width), F32)
        for k in range(taps):
            begin = 8 - (taps - 1) + k
            preact = preact + weight[k : k + 1, :] * padded[s, begin : begin + tokens, :]
        rows = slice(s * tokens, (s + 1) * tokens)
        preact_out[rows, :] = preact
        xconv_out[rows, :] = (preact * lax.logistic(preact)).astype(BF16)
    x_flat = xconv_out[...]
    rank = dt_out.shape[0]
    low_out[...] = dot_nt(x_flat, proj[:rank]).reshape(low_out.shape).astype(BF16)
    bc = dot_nt(proj[rank:], x_flat)
    per = bc_out.shape[1]
    for e in range(bc_out.shape[0]):
        bc_out[e] = bc[e * per : (e + 1) * per, :]


def decay_of(step_row, rate):
    return jnp.exp(step_row * rate)


def views(refs, first, count, lanes):
    first = pl.multiple_of(first, count)
    return [ref.at[pl.ds(first, count), lanes] for ref in refs]


def local_body(
    low_all, bc_all, dt_weight, dt_bias, a_log, xconv, zin, cot,
    pre_out, step_out, gy_out, bx_out, cx_out, parts_out, bc_rows, u_rows,
):
    seqs, tokens, width = zin.shape
    states = a_log.shape[0]
    rows = seqs * tokens
    low = low_all[...].reshape(rows, low_all.shape[2])
    pre = dot_nn(low, dt_weight[...]) + dt_bias[...]
    pre_out[...] = pre
    step = jnp.maximum(pre, 0.0) + jnp.log1p(jnp.exp(-jnp.abs(pre)))
    step_out[...] = step
    u_rows[...] = step * xconv[...].astype(F32)
    per = bc_all.shape[1]
    for e in range(bc_all.shape[0]):
        bc_rows[e * per : (e + 1) * per, :] = bc_all[e]
    for s in range(seqs):
        z = zin[s].astype(F32)
        gy_out[s * tokens : (s + 1) * tokens, :] = cot[s].astype(F32) * z * lax.logistic(z)
    for r in range(rows):
        bx_out[r] = jnp.broadcast_to(bc_rows[0:states, r : r + 1], (states, LANES))
        cx_out[r] = jnp.broadcast_to(bc_rows[states : 2 * states, r : r + 1], (states, LANES))
    rate_all = -jnp.exp(a_log[...])
    chunk = 8
    for block in range(width // LANES):
        lanes = slice(block * LANES, (block + 1) * LANES)
        rate = rate_all[:, lanes]

        def one(k, carried):
            ahead = list(carried[:seqs])
            behind = list(carried[seqs:])
            for s in range(seqs):
                first = s * tokens + k * chunk
                last = s * tokens + tokens - (k + 1) * chunk
                step_f, u_f = views((step_out, u_rows), first, chunk, lanes)
                step_b, gy_b = views((step_out, gy_out), last, chunk, lanes)
                for i in range(chunk):
                    now = decay_of(step_f[i : i + 1, :], rate)
                    ahead[s] = now * ahead[s] + bx_out[first + i] * u_f[i : i + 1, :]
                    j = chunk - 1 - i
                    now = decay_of(step_b[j : j + 1, :], rate)
                    behind[s] = now * (cx_out[last + j] * gy_b[j : j + 1, :] + behind[s])
            return tuple(ahead + behind)

        zero = jnp.zeros((states, LANES), F32)
        ends = lax.fori_loop(0, tokens // chunk, one, (zero,) * (2 * seqs))
        for s in range(seqs):
            total = jnp.sum(step[s * tokens : (s + 1) * tokens, lanes], axis=0, keepdims=True)
            passing = jnp.exp(rate * total)
            for n in range(states):
                parts_out[s * states + n, 0:1, lanes] = ends[s][n : n + 1, :]
                parts_out[s * states + n, 1:2, lanes] = ends[seqs + s][n : n + 1, :]
                parts_out[s * states + n, 2:3, lanes] = passing[n : n + 1, :]


def main_body(
    step, pre, xconv, gy, zin, cot, bx, cx, bc_all, a_log, d_skip, incoming, dt_weight, low_all,
    gate_out, low_out, bc_out, dtw_out, base_out, sums_out,
    bc_rows, begin, hist, adjoint, prevs, u_rows, y_rows, b_rows, q_rows, fold_b, fold_c,
):
    seqs, tokens, width = zin.shape
    states = a_log.shape[0]
    rows = seqs * tokens
    span = CHUNK * states
    turns = tokens // CHUNK
    per = bc_all.shape[1]
    for e in range(bc_all.shape[0]):
        bc_rows[e * per : (e + 1) * per, :] = bc_all[e]
    for s in range(seqs):
        for n in range(states):
            begin[s, n : n + 1, :] = incoming[s * states + n, 0:1, :]
            begin[seqs + s, n : n + 1, :] = incoming[s * states + n, 1:2, :]
        hist[s, 0] = begin[s].astype(BF16)
    u_rows[...] = step[...] * xconv[...].astype(F32)
    rate_all = -jnp.exp(a_log[...])
    spread = (
        (lax.broadcasted_iota(jnp.int32, (states, span), 1) & (states - 1))
        == lax.broadcasted_iota(jnp.int32, (states, span), 0)
    ).astype(F32)
    spread_half = spread.astype(BF16)
    own = (
        lax.broadcasted_iota(jnp.int32, (rows, span), 1) // states
        == (lax.broadcasted_iota(jnp.int32, (rows, span), 0) & (CHUNK - 1))
    ).astype(F32)
    across = jnp.transpose(bc_rows[...])
    b_diag = (dot_nn(across[:, :states].astype(BF16), spread_half) * own).astype(BF16)
    c_diag = (dot_nn(across[:, states:].astype(BF16), spread_half) * own).astype(BF16)
    fold = own[:CHUNK].astype(BF16)
    gy_half = gy[...].astype(BF16)
    u_half = u_rows[...].astype(BF16)

    for block in range(width // LANES):
        lanes = slice(block * LANES, (block + 1) * LANES)
        rate = rate_all[:, lanes]

        def forward(k, carried):
            carried = list(carried)
            t = k * CHUNK
            for s in range(seqs):
                step_v, u_v = views((step, u_rows), s * tokens + t, CHUNK, lanes)
                for i in range(CHUNK):
                    now = decay_of(step_v[i : i + 1, :], rate)
                    carried[s] = now * carried[s] + bx[s * tokens + t + i] * u_v[i : i + 1, :]
                    hist[s, t + i + 1, :, lanes] = carried[s].astype(BF16)
            return tuple(carried)

        lax.fori_loop(0, turns, forward, tuple(begin[s, :, lanes] for s in range(seqs)))

        def backward(k, carried):
            passed = list(carried[:seqs])
            rate_grad = carried[seqs]
            first = tokens - (k + 1) * CHUNK
            for s in range(seqs):
                step_v, gy_v = views((step, gy), s * tokens + first, CHUNK, lanes)
                for i in reversed(range(CHUNK)):
                    t = first + i
                    step_row = step_v[i : i + 1, :]
                    now = decay_of(step_row, rate)
                    adj = cx[s * tokens + t] * gy_v[i : i + 1, :] + passed[s]
                    adjoint[s, t, :, lanes] = adj.astype(BF16)
                    passed[s] = now * adj
                    prev = passed[s] * hist[s, t, :, lanes].astype(F32) * rate
                    prevs[s, t, :, lanes] = prev.astype(BF16)
                    rate_grad = rate_grad + prev * step_row
            return tuple(passed) + (rate_grad,)

        ends = lax.fori_loop(
            0,
            turns,
            backward,
            tuple(begin[seqs + s, :, lanes] for s in range(seqs))
            + (jnp.zeros((states, LANES), F32),),
        )
        sums_out[0:states, lanes] = ends[seqs]

    for s in range(seqs):
        for k in range(turns):
            t = k * CHUNK
            here = slice(s * tokens + t, s * tokens + t + CHUNK)
            history = hist[s, t + 1 : t + 1 + CHUNK].reshape(span, width)
            y_rows[here, :] = dot_nn(c_diag[here], history)
            fold_c[here, :] = dot_nt(gy_half[here], history) * own[:CHUNK]
            adj = adjoint[s, t : t + CHUNK].reshape(span, width)
            b_rows[here, :] = dot_nn(b_diag[here], adj)
            fold_b[here, :] = dot_nt(u_half[here], adj) * own[:CHUNK]
            q_rows[here, :] = dot_nn(fold, prevs[s, t : t + CHUNK].reshape(span, width))

    exact = lax.Precision.HIGHEST
    grad_b = dot_nt(spread, fold_b[...], exact)
    grad_c = dot_nt(spread, fold_c[...], exact)
    grad_bc = jnp.concatenate([grad_b, grad_c], 0)
    for e in range(bc_out.shape[0]):
        bc_out[e] = grad_bc[e * per : (e + 1) * per, :]

    x = xconv[...].astype(F32)
    for s in range(seqs):
        here = slice(s * tokens, (s + 1) * tokens)
        z = zin[s].astype(F32)
        sig = lax.logistic(z)
        y_value = y_rows[here, :] + d_skip[...] * x[here]
        gate_out[s] = (cot[s].astype(F32) * y_value * sig * (1.0 + z * (1.0 - sig))).astype(BF16)
    b_adjoint = b_rows[...]
    grad_pre = (x * b_adjoint + q_rows[...]) * lax.logistic(pre[...])
    grad_round = grad_pre.astype(BF16)
    base_out[...] = d_skip[...] * gy[...] + step[...] * b_adjoint
    low_out[...] = dot_nt(grad_round, dt_weight[...]).reshape(low_out.shape).astype(BF16)
    low = low_all[...].reshape(rows, low_all.shape[2])
    dtw_out[...] = dot_tn(low, grad_round)
    sums_out[states : states + 1, :] = jnp.sum(grad_pre, axis=0, keepdims=True)
    sums_out[states + 1 : states + 2, :] = jnp.sum(gy[...] * x, axis=0, keepdims=True)


def last_body(
    low_all, bc_all, xconv, proj, base, preact, xin, front, weight, dtw, sums,
    big_out, small_out, edge_out, gradx_out, tail_out, padded, grads, bc_rows,
):
    seqs, tokens, width = xin.shape
    taps = weight.shape[0]
    reach = taps - 1
    rows = seqs * tokens
    rank = low_all.shape[2]
    per = bc_all.shape[1]
    for e in range(bc_all.shape[0]):
        bc_rows[e * per : (e + 1) * per, :] = bc_all[e]
    low = low_all[...].reshape(rows, rank)
    bc = bc_rows[...].astype(BF16)
    x_flat = xconv[...]
    low_terms = dot_tn(low, x_flat)
    for i in range(big_out.shape[0]):
        part = big_out.shape[1] // 2
        big_out[i] = jnp.concatenate(
            [low_terms[i * part : (i + 1) * part], dtw[i * part : (i + 1) * part, :]], 0
        ).astype(BF16)
    state_terms = dot_nn(bc, x_flat)
    across = jnp.transpose(bc_rows[...]).astype(BF16)
    grad_conv = base[...] + dot_nn(low, proj[0:rank, :]) + dot_nn(across, proj[rank:, :])
    pre = preact[...]
    sig = lax.logistic(pre)
    grad_pre = grad_conv * sig * (1.0 + pre * (1.0 - sig))
    keep = jnp.where(lax.axis_index("dp") == 0, 0.0, 1.0).astype(F32)
    lead = front[...].astype(F32) * keep
    conv_terms = [jnp.zeros((1, width), F32) for k in range(taps)]
    edge_out[...] = jnp.zeros(edge_out.shape, F32)
    tail_out[...] = jnp.zeros(tail_out.shape, F32)
    for s in range(seqs):
        mine = grad_pre[s * tokens : (s + 1) * tokens]
        padded[s, 8 - reach : 8, :] = lead[s * reach : (s + 1) * reach, :]
        padded[s, 8:, :] = xin[s].astype(F32)
        grads[s, 0:tokens, :] = mine
        grads[s, tokens:, :] = jnp.zeros((8, width), F32)
        edge_out[s * reach : (s + 1) * reach, :] = mine[0:reach]
        result = jnp.zeros((tokens, width), F32)
        for k in range(taps):
            begin = 8 - reach + k
            conv_terms[k] = conv_terms[k] + jnp.sum(
                mine * padded[s, begin : begin + tokens, :], axis=0, keepdims=True
            )
            late = reach - k
            result = result + weight[k : k + 1, :] * grads[s, late : late + tokens, :]
        gradx_out[s] = result.astype(BF16)
        tail_out[s * reach : (s + 1) * reach, :] = result[tokens - reach :]
    states2 = bc.shape[0]
    extra = sums.shape[0]
    pieces = [state_terms[i : i + 1] for i in range(states2)]
    pieces += conv_terms
    pieces.append(jnp.sum(grad_pre, axis=0, keepdims=True))
    pieces += [sums[i : i + 1, :] for i in range(extra)]
    while len(pieces) < 2 * small_out.shape[0]:
        pieces.append(jnp.zeros((1, width), F32))
    for i, piece in enumerate(pieces):
        small_out[i // 2, i % 2 : i % 2 + 1, :] = piece


def body(
    xin, zin, cotangent, conv_weight, conv_bias, proj_weight, dt_weight, dt_bias, a_log, d_skip
):
    dp = lax.axis_size("dp")
    expert = lax.axis_size("expert")
    seqs, tokens, width = xin.shape
    taps = conv_weight.shape[0]
    reach = taps - 1
    states = a_log.shape[0]
    rows = seqs * tokens
    low_rows = dt_weight.shape[0]
    proj_rows = proj_weight.shape[0]
    rank = low_rows * dp
    total_rows = proj_rows * dp

    block = jnp.concatenate([dt_weight, proj_weight[:low_rows]], 0)
    extra = proj_weight[low_rows:].astype(F32)
    edge = jnp.pad(
        xin[:, tokens - reach :, :].reshape(seqs * reach, width), ((0, 16 - seqs * reach), (0, 0))
    )
    block_all, extra_all, front = gather_weights(block, extra, edge, dp)

    pick_dt = np.zeros((rank, 2 * rank), np.float32)
    pick_low = np.zeros((total_rows, 2 * rank), np.float32)
    pick_extra = np.zeros((total_rows, dp), np.float32)
    for i in range(dp):
        for j in range(low_rows):
            pick_dt[i * low_rows + j, i * 2 * low_rows + j] = 1.0
            pick_low[i * proj_rows + j, i * 2 * low_rows + low_rows + j] = 1.0
        pick_extra[i * proj_rows + low_rows, i] = 1.0

    low_shape = (expert, rows // expert, rank)
    bc_shape = (expert, 2 * states // expert, rows)
    flat = (rows, width)
    preact, xconv, low_part, bc_part, proj_full, dt_full = local_call(
        conv_body,
        (
            sds(flat, F32),
            sds(flat, BF16),
            sds(low_shape, BF16),
            sds(bc_shape, F32),
            sds((total_rows, width), BF16),
            sds((rank, width), BF16),
        ),
        [pltpu.VMEM((seqs, tokens + 8, width), F32), pltpu.VMEM((dp, width), F32)],
        "conv_project",
        xin,
        front,
        block_all,
        extra_all,
        jnp.asarray(pick_dt, BF16),
        jnp.asarray(pick_low, BF16),
        jnp.asarray(pick_extra, BF16),
        conv_weight,
        conv_bias[None, :],
    )
    low_all, bc_all = reduce_expert(low_part, bc_part, expert, 2)

    wide = (rows, states, LANES)
    pre, step, gy, bx, cx, parts = local_call(
        local_body,
        (
            sds(flat, F32),
            sds(flat, F32),
            sds(flat, F32),
            sds(wide, F32),
            sds(wide, F32),
            sds((seqs * states, 3, width), F32),
        ),
        [pltpu.VMEM((2 * states, rows), F32), pltpu.VMEM(flat, F32)],
        "local_scans",
        low_all,
        bc_all,
        dt_full,
        dt_bias[None, :],
        a_log,
        xconv,
        zin,
        cotangent,
    )
    incoming = exchange_carries(parts, dp)

    gate, low_grad, bc_grad, dtw, base, sums = local_call(
        main_body,
        (
            sds((seqs, tokens, width), BF16),
            sds(low_shape, BF16),
            sds(bc_shape, F32),
            sds((rank, width), F32),
            sds(flat, F32),
            sds((states + 2, width), F32),
        ),
        [
            pltpu.VMEM((2 * states, rows), F32),
            pltpu.VMEM((2 * seqs, states, width), F32),
            pltpu.VMEM((seqs, tokens + 1, states, width), BF16),
            pltpu.VMEM((seqs, tokens, states, width), BF16),
            pltpu.VMEM((seqs, tokens, states, width), BF16),
            pltpu.VMEM(flat, F32),
            pltpu.VMEM(flat, F32),
            pltpu.VMEM(flat, F32),
            pltpu.VMEM(flat, F32),
            pltpu.VMEM((rows, CHUNK * states), F32),
            pltpu.VMEM((rows, CHUNK * states), F32),
        ],
        "full_scans",
        step,
        pre,
        xconv,
        gy,
        zin,
        cotangent,
        bx,
        cx,
        bc_all,
        a_log,
        d_skip[None, :],
        incoming,
        dt_full,
        low_all,
    )
    low_sum, bc_sum = reduce_expert(low_grad, bc_grad, expert, 4)

    big, small, edge_grad, grad_x, tail = local_call(
        last_body,
        (
            sds((dp, 2 * low_rows, width), BF16),
            sds((dp, 2, width), F32),
            sds((8, width), F32),
            sds((seqs, tokens, width), BF16),
            sds((8, width), F32),
        ),
        [
            pltpu.VMEM((seqs, tokens + 8, width), F32),
            pltpu.VMEM((seqs, tokens + 8, width), F32),
            pltpu.VMEM((2 * states, rows), F32),
        ],
        "weight_grads",
        low_sum,
        bc_sum,
        xconv,
        proj_full,
        base,
        preact,
        xin,
        front,
        conv_weight,
        dtw,
        sums,
    )
    grad_low, grad_dtw, small_all, after = finish_sums(big, small, edge_grad, dp)

    after = jnp.where(lax.axis_index("dp") == dp - 1, 0.0, after)
    after = after[: seqs * reach].reshape(seqs, reach, width)
    ends = tail[: seqs * reach].reshape(seqs, reach, width)
    fixed = []
    for i in range(reach):
        row = ends[:, i]
        for k in range(taps):
            source = i + (reach - k) - reach
            if source >= 0:
                row = row + conv_weight[k][None, :] * after[:, source]
        fixed.append(row)
    grad_x = lax.dynamic_update_slice(
        grad_x, jnp.stack(fixed, 1).astype(BF16), (0, tokens - reach, 0)
    )
    table = small_all.reshape(2 * dp, width)
    at = 2 * states
    return (
        grad_x,
        gate,
        grad_low,
        table[:at],
        grad_dtw,
        table[at : at + taps],
        table[at + taps],
        table[at + taps + 1 + states],
        table[at + taps + 1 : at + taps + 1 + states],
        table[at + taps + 2 + states],
    )


def solution(mesh):
    return jax.shard_map(
        body,
        mesh=mesh,
        in_specs=(
            P(None, "dp", "expert"),
            P(None, "dp", "expert"),
            P(None, "dp", "expert"),
            P(None, "expert"),
            P("expert"),
            P("dp", "expert"),
            P("dp", "expert"),
            P("expert"),
            P(None, "expert"),
            P("expert"),
        ),
        out_specs=(
            P(None, "dp", "expert"),
            P(None, "dp", "expert"),
            P("dp", "expert"),
            P(None, "expert"),
            P("dp", "expert"),
            P(None, "expert"),
            P("expert"),
            P("expert"),
            P(None, "expert"),
            P("expert"),
        ),
        check_vma=False,
    )
```

```python
import functools

import jax
import jax.numpy as jnp
from jax import lax
from jax.experimental import pallas as pl
from jax.experimental.pallas import tpu as pltpu
from jax.sharding import PartitionSpec as P

F32 = jnp.float32
BF16 = jnp.bfloat16
MESH = pl.DeviceIdType.MESH
LANES = 128
CHUNK = 16
VMEM_BYTES = 56 * 1024 * 1024

whole = pl.BlockSpec(memory_space=pltpu.VMEM)
sds = jax.ShapeDtypeStruct


def dot_nn(left, right, precision=None):
    return lax.dot_general(
        left, right, (((1,), (0,)), ((), ())), preferred_element_type=F32, precision=precision
    )


def dot_nt(left, right, precision=None):
    return lax.dot_general(
        left, right, (((1,), (1,)), ((), ())), preferred_element_type=F32, precision=precision
    )


def dot_tn(left, right):
    return lax.dot_general(left, right, (((0,), (0,)), ((), ())), preferred_element_type=F32)


def hail(axis, count, me):
    barrier = pltpu.get_barrier_semaphore()

    def one(k, carry):
        pl.semaphore_signal(
            barrier, inc=1, device_id={axis: lax.rem(me + k, count)}, device_id_type=MESH
        )
        return carry

    lax.fori_loop(1, count, one, 0)


def send_all(axis, count, me, source, landing, send_sem, recv_sem):
    def one(k, carry):
        peer = lax.rem(me + k, count)
        pltpu.make_async_remote_copy(
            src_ref=source(peer),
            dst_ref=landing(me),
            send_sem=send_sem.at[k],
            recv_sem=recv_sem.at[k],
            device_id={axis: peer},
            device_id_type=MESH,
        ).start()
        return carry

    lax.fori_loop(1, count, one, 0)


def wait_all(axis, count, me, source, landing, send_sem, recv_sem, sent):
    def one(k, carry):
        peer = lax.rem(me + k, count)
        origin = lax.rem(me + count - k, count)
        copy = pltpu.make_async_remote_copy(
            src_ref=source(peer),
            dst_ref=landing(origin),
            send_sem=send_sem.at[k],
            recv_sem=recv_sem.at[k],
            device_id={axis: peer},
            device_id_type=MESH,
        )
        if sent:
            copy.wait_send()
        else:
            copy.wait_recv()
        return carry

    lax.fori_loop(1, count, one, 0)


class Exchange:
    def __init__(self, axis, count, me, source, landing, sems):
        self.args = (axis, count, me, source, landing, sems[0], sems[1])

    def start(self):
        send_all(*self.args)

    def wait_recv(self):
        wait_all(*self.args, False)

    def wait_send(self):
        wait_all(*self.args, True)


def fold_lanes(value):
    half = value.shape[1] // 2
    return jnp.concatenate([value[:, :half], value[:, half:]], 0)


def unfold_lanes(value):
    half = value.shape[0] // 2
    return jnp.concatenate([value[:half], value[half:]], 1)


def views(refs, first, count, lanes):
    first = pl.multiple_of(first, count)
    return [ref.at[pl.ds(first, count), lanes] for ref in refs]


def reduce_start(ex_low, ex_bc, low_slots, bc_slots, low, bc, me):
    ex_low.start()
    ex_bc.start()
    low_slots[me] = low[me]
    bc_slots[me] = bc[me]


def reduce_middle(ex, low_slots, bc_slots, low_all, bc_all, me, count):
    ex[0].wait_recv()
    ex[1].wait_recv()

    def add(k, total):
        return (total[0] + low_slots[k].astype(F32), total[1] + bc_slots[k])

    zero = (jnp.zeros(low_slots.shape[1:], F32), jnp.zeros(bc_slots.shape[1:], F32))
    low_sum, bc_sum = lax.fori_loop(0, count, add, zero)
    low_all[me] = low_sum.astype(BF16)
    bc_all[me] = bc_sum
    ex[2].start()
    ex[3].start()


def spread_rows(source, target):
    per = source.shape[1]
    for e in range(source.shape[0]):
        target[e * per : (e + 1) * per, :] = source[e]


def core_body(
    dp, expert,
    xin, zin, cot, conv_weight, conv_bias, proj_mine, dt_mine, dt_bias, a_log, d_skip,
    gate_out, gradx_out, proj_out, dtw_out, small_all,
    send_proj, send_extra, send_dt, send_edge, all_proj, all_extra, all_dt, front,
    low_part, bc_part, low_slots, bc_slots, low_all, bc_all,
    low_part2, bc_part2, low_slots2, bc_slots2, low_all2, bc_all2,
    parts, slots, found, incoming,
    dtw_part, dtw_slots, pw_part, pw_slots, small_part, small_slots, edge_grad, after,
    proj_wide, proj_full, dt_full, padded, grads, preact, xconv, pre, step, gy, gate_factor,
    u_rows, y_rows, b_rows, q_rows, fold_b, fold_c, bx, cx, bc_rows, begin, hist, adjoint, prevs,
    *sems,
):
    seqs, tokens, width = zin.shape
    states = a_log.shape[0]
    taps = conv_weight.shape[0]
    reach = taps - 1
    rows = seqs * tokens
    rank = dt_full.shape[0]
    part = dt_mine.shape[0]
    proj_rows = proj_mine.shape[0]
    me = lax.axis_index("dp")
    mine = lax.axis_index("expert")
    hail("dp", dp, me)
    hail("expert", expert, mine)

    pairs = iter(range(0, len(sems), 2))

    def next_pair():
        i = next(pairs)
        return (sems[i], sems[i + 1])

    def over_dp(source, landing):
        return Exchange("dp", dp, me, source, landing, next_pair())

    def over_expert(source, landing):
        return Exchange("expert", expert, mine, source, landing, next_pair())

    def reduction(low, bc, low_in, bc_in, low_out, bc_out):
        return (
            over_expert(lambda p: low.at[p], lambda d: low_in.at[d]),
            over_expert(lambda p: bc.at[p], lambda d: bc_in.at[d]),
            over_expert(lambda p: low_out.at[mine], lambda d: low_out.at[d]),
            over_expert(lambda p: bc_out.at[mine], lambda d: bc_out.at[d]),
        )

    ex_proj = over_dp(lambda p: send_proj, lambda d: all_proj.at[d])
    ex_extra = over_dp(lambda p: send_extra, lambda d: all_extra.at[d])
    ex_dt = over_dp(lambda p: send_dt, lambda d: all_dt.at[d])
    ex_one = reduction(low_part, bc_part, low_slots, bc_slots, low_all, bc_all)
    ex_two = reduction(low_part2, bc_part2, low_slots2, bc_slots2, low_all2, bc_all2)
    ex_parts = over_dp(lambda p: parts.at[p], lambda d: slots.at[d])
    ex_found = over_dp(lambda p: found.at[p], lambda d: incoming.at[d])
    ex_dtw = over_dp(lambda p: dtw_part.at[p], lambda d: dtw_slots.at[d])
    ex_pw = over_dp(lambda p: pw_part.at[p], lambda d: pw_slots.at[d])
    ex_small = over_dp(lambda p: small_part.at[p], lambda d: small_slots.at[d])
    ex_total = over_dp(lambda p: small_all.at[me], lambda d: small_all.at[d])

    def neighbour(source, target, distance):
        pair = next_pair()
        return pltpu.make_async_remote_copy(
            src_ref=source,
            dst_ref=target,
            send_sem=pair[0],
            recv_sem=pair[1],
            device_id={"dp": lax.rem(me + dp + distance, dp)},
            device_id_type=MESH,
        )

    halo = neighbour(send_edge, front, 1)
    halo_back = neighbour(edge_grad, after, -1)

    proj32 = proj_mine[...].astype(F32)
    send_proj[...] = fold_lanes(proj32[:part]).astype(BF16)
    send_extra[...] = proj32[part:]
    send_dt[...] = fold_lanes(dt_mine[...].astype(F32)).astype(BF16)
    send_edge[...] = jnp.concatenate(
        [xin[s, tokens - 16 :, :].astype(F32)[8:] for s in range(seqs)], 0
    ).astype(BF16)
    all_proj[me] = send_proj[...]
    all_extra[me] = send_extra[...]
    all_dt[me] = send_dt[...]
    for s in range(seqs):
        here = slice(s * tokens, (s + 1) * tokens)
        z = zin[s].astype(F32)
        g = cot[s].astype(F32)
        sig = lax.logistic(z)
        gy[here, :] = g * z * sig
        gate_factor[here, :] = g * sig * (1.0 + z * (1.0 - sig))
        padded[s, 8:, :] = xin[s].astype(F32)
    rate_all = -jnp.exp(a_log[...])
    pl.semaphore_wait(pltpu.get_barrier_semaphore(), dp + expert - 2)

    halo.start()
    ex_proj.start()
    ex_extra.start()
    ex_dt.start()

    halo.wait_recv()
    keep = jnp.where(me == 0, 0.0, 1.0).astype(F32)
    lead = front[...].astype(F32) * keep
    for s in range(seqs):
        padded[s, 8 - reach : 8, :] = lead[8 * s + 8 - reach : 8 * s + 8, :]
        value = conv_bias[...] + jnp.zeros((tokens, width), F32)
        for k in range(taps):
            first = 8 - reach + k
            value = value + conv_weight[k : k + 1, :] * padded[s, first : first + tokens, :]
        here = slice(s * tokens, (s + 1) * tokens)
        preact[here, :] = value
        xconv[here, :] = (value * lax.logistic(value)).astype(BF16)
    ex_proj.wait_recv()
    ex_extra.wait_recv()
    for i in range(dp):
        proj_wide[i * proj_rows : i * proj_rows + part, :] = unfold_lanes(all_proj[i].astype(F32))
        proj_wide[i * proj_rows + part : (i + 1) * proj_rows, :] = all_extra[i]
    proj_full[...] = proj_wide[...].astype(BF16)
    x_flat = xconv[...]
    bc = dot_nt(proj_full[rank:, :], x_flat)
    per = bc_part.shape[1]
    for e in range(expert):
        bc_part[e] = bc[e * per : (e + 1) * per, :]
    low_part[...] = dot_nt(x_flat, proj_full[0:rank, :]).reshape(low_part.shape).astype(BF16)
    reduce_start(ex_one[0], ex_one[1], low_slots, bc_slots, low_part, bc_part, mine)
    ex_dt.wait_recv()
    for i in range(0, dp, 2):
        pair = [unfold_lanes(all_dt[i + j].astype(F32)) for j in range(2)]
        dt_full[i * part : (i + 2) * part, :] = jnp.concatenate(pair, 0).astype(BF16)
    reduce_middle(ex_one, low_slots, bc_slots, low_all, bc_all, mine, expert)
    ex_one[3].wait_recv()
    spread_rows(bc_all, bc_rows)
    for r in range(rows):
        bx[r] = jnp.broadcast_to(bc_rows[0:states, r : r + 1], (states, LANES))
        cx[r] = jnp.broadcast_to(bc_rows[states : 2 * states, r : r + 1], (states, LANES))
    ex_one[2].wait_recv()
    low = low_all[...].reshape(rows, rank)
    pre_value = dot_nn(low, dt_full[...]) + dt_bias[...]
    pre[...] = pre_value
    step_value = jnp.maximum(pre_value, 0.0) + jnp.log1p(jnp.exp(-jnp.abs(pre_value)))
    step[...] = step_value
    u_rows[...] = step_value * xconv[...].astype(F32)

    for block in range(width // LANES):
        lanes = slice(block * LANES, (block + 1) * LANES)
        rate = rate_all[:, lanes]

        def alone(k, carried):
            ahead = list(carried[:seqs])
            behind = list(carried[seqs:])
            for s in range(seqs):
                first = s * tokens + k * 8
                last = s * tokens + tokens - (k + 1) * 8
                step_f, u_f = views((step, u_rows), first, 8, lanes)
                step_b, gy_b = views((step, gy), last, 8, lanes)
                for i in range(8):
                    now = jnp.exp(step_f[i : i + 1, :] * rate)
                    ahead[s] = now * ahead[s] + bx[first + i] * u_f[i : i + 1, :]
                    j = 7 - i
                    now = jnp.exp(step_b[j : j + 1, :] * rate)
                    behind[s] = now * (cx[last + j] * gy_b[j : j + 1, :] + behind[s])
            return tuple(ahead + behind)

        zero = jnp.zeros((states, LANES), F32)
        ends = lax.fori_loop(0, tokens // 8, alone, (zero,) * (2 * seqs))
        for s in range(seqs):
            total = jnp.sum(step[s * tokens : (s + 1) * tokens, lanes], axis=0, keepdims=True)
            passing = jnp.exp(rate * total)
            for n in range(states):
                parts[s * states + n, 0:1, lanes] = ends[s][n : n + 1, :]
                parts[s * states + n, 1:2, lanes] = ends[seqs + s][n : n + 1, :]
                parts[s * states + n, 2:3, lanes] = passing[n : n + 1, :]

    ex_parts.start()
    slots[me] = parts[me]
    span = CHUNK * states
    turns = tokens // CHUNK
    spread = (
        (lax.broadcasted_iota(jnp.int32, (states, span), 1) & (states - 1))
        == lax.broadcasted_iota(jnp.int32, (states, span), 0)
    ).astype(F32)
    spread_half = spread.astype(BF16)
    own = (
        lax.shift_right_logical(
            lax.broadcasted_iota(jnp.int32, (rows, span), 1), states.bit_length() - 1
        )
        == (lax.broadcasted_iota(jnp.int32, (rows, span), 0) & (CHUNK - 1))
    ).astype(F32)
    across = jnp.transpose(bc_rows[...])
    b_diag = (dot_nn(across[:, :states].astype(BF16), spread_half) * own).astype(BF16)
    c_diag = (dot_nn(across[:, states:].astype(BF16), spread_half) * own).astype(BF16)
    own = own[:CHUNK]
    fold = own.astype(BF16)
    ex_parts.wait_recv()

    def prefix(k, carried):
        ahead, behind = carried
        late = dp - 1 - k
        found[k, 0:1, :] = ahead
        found[late, 1:2, :] = behind
        ahead = slots[k, 2:3, :] * ahead + slots[k, 0:1, :]
        behind = slots[late, 2:3, :] * behind + slots[late, 1:2, :]
        return (ahead, behind)

    zero = jnp.zeros((1, width), F32)
    lax.fori_loop(0, dp, prefix, (zero, zero))
    ex_found.start()
    incoming[me] = found[me]
    gy_half = gy[...].astype(BF16)
    u_half = u_rows[...].astype(BF16)
    ex_found.wait_recv()
    for s in range(seqs):
        for n in range(states):
            begin[s, n : n + 1, :] = incoming[s * states + n, 0:1, :]
            begin[seqs + s, n : n + 1, :] = incoming[s * states + n, 1:2, :]
        hist[s, 0] = begin[s].astype(BF16)

    rate_sums = []
    for block in range(width // LANES):
        lanes = slice(block * LANES, (block + 1) * LANES)
        rate = rate_all[:, lanes]

        def forward(k, carried):
            carried = list(carried)
            t = k * CHUNK
            for s in range(seqs):
                step_v, u_v = views((step, u_rows), s * tokens + t, CHUNK, lanes)
                for i in range(CHUNK):
                    now = jnp.exp(step_v[i : i + 1, :] * rate)
                    carried[s] = now * carried[s] + bx[s * tokens + t + i] * u_v[i : i + 1, :]
                    hist[s, t + i + 1, :, lanes] = carried[s].astype(BF16)
            return tuple(carried)

        lax.fori_loop(0, turns, forward, tuple(begin[s, :, lanes] for s in range(seqs)))

        def backward(k, carried):
            passed = list(carried[:seqs])
            rate_grad = list(carried[seqs:])
            first = tokens - (k + 1) * CHUNK
            for s in range(seqs):
                step_v, gy_v = views((step, gy), s * tokens + first, CHUNK, lanes)
                for i in reversed(range(CHUNK)):
                    t = first + i
                    step_row = step_v[i : i + 1, :]
                    now = jnp.exp(step_row * rate)
                    adj = cx[s * tokens + t] * gy_v[i : i + 1, :] + passed[s]
                    adjoint[s, t, :, lanes] = adj.astype(BF16)
                    passed[s] = now * adj
                    prev = passed[s] * hist[s, t, :, lanes].astype(F32) * rate
                    prevs[s, t, :, lanes] = prev.astype(BF16)
                    rate_grad[s] = rate_grad[s] + prev * step_row
            return tuple(passed + rate_grad)

        ends = lax.fori_loop(
            0,
            turns,
            backward,
            tuple(begin[seqs + s, :, lanes] for s in range(seqs))
            + (jnp.zeros((states, LANES), F32),) * seqs,
        )
        rate_sums.append(sum(ends[seqs + 1 :], ends[seqs]))

    for s in range(seqs):
        for k in range(turns):
            t = k * CHUNK
            here = slice(s * tokens + t, s * tokens + t + CHUNK)
            history = hist[s, t + 1 : t + 1 + CHUNK].reshape(span, width)
            y_rows[here, :] = dot_nn(c_diag[here], history)
            fold_c[here, :] = dot_nt(gy_half[here], history) * own
            adj = adjoint[s, t : t + CHUNK].reshape(span, width)
            b_rows[here, :] = dot_nn(b_diag[here], adj)
            fold_b[here, :] = dot_nt(u_half[here], adj) * own
            q_rows[here, :] = dot_nn(fold, prevs[s, t : t + CHUNK].reshape(span, width))

    exact = lax.Precision.HIGHEST
    grad_b = dot_nt(spread, fold_b[...], exact)
    grad_c = dot_nt(spread, fold_c[...], exact)
    grad_bc = jnp.concatenate([grad_b, grad_c], 0)
    for e in range(expert):
        bc_part2[e] = grad_bc[e * per : (e + 1) * per, :]
    x = xconv[...].astype(F32)
    b_adjoint = b_rows[...]
    grad_pre = (x * b_adjoint + q_rows[...]) * lax.logistic(pre[...])
    grad_round = grad_pre.astype(BF16)
    low_part2[...] = dot_nt(grad_round, dt_full[...]).reshape(low_part.shape).astype(BF16)
    reduce_start(ex_two[0], ex_two[1], low_slots2, bc_slots2, low_part2, bc_part2, mine)

    dtw = dot_tn(low_all[...].reshape(rows, rank), grad_round)
    for i in range(dp):
        dtw_part[i] = fold_lanes(dtw[i * part : (i + 1) * part]).astype(BF16)
    ex_dtw.start()
    dtw_slots[me] = dtw_part[me]
    sums = [jnp.concatenate(rate_sums, 1)]
    sums.append(jnp.sum(grad_pre, axis=0, keepdims=True))
    sums.append(jnp.sum(gy[...] * x, axis=0, keepdims=True))
    y_value = y_rows[...] + d_skip[...] * x
    gate_out[...] = (y_value * gate_factor[...]).astype(BF16).reshape(gate_out.shape)
    b_rows[...] = d_skip[...] * gy[...] + step[...] * b_adjoint
    reduce_middle(ex_two, low_slots2, bc_slots2, low_all2, bc_all2, mine, expert)
    ex_two[2].wait_recv()
    ex_two[3].wait_recv()

    spread_rows(bc_all2, bc_rows)
    low2 = low_all2[...].reshape(rows, rank)
    x_flat = xconv[...]
    pw = dot_tn(low2, x_flat)
    for i in range(dp):
        pw_part[i] = fold_lanes(pw[i * part : (i + 1) * part]).astype(BF16)
    ex_pw.start()
    pw_slots[me] = pw_part[me]
    state_terms = dot_nn(bc_rows[...].astype(BF16), x_flat)
    across = jnp.transpose(bc_rows[...]).astype(BF16)
    grad_conv = (
        b_rows[...] + dot_nn(low2, proj_full[0:rank, :]) + dot_nn(across, proj_full[rank:, :])
    )
    value = preact[...]
    sig = lax.logistic(value)
    grad_pre = grad_conv * sig * (1.0 + value * (1.0 - sig))
    conv_terms = [jnp.zeros((1, width), F32) for k in range(taps)]
    for s in range(seqs):
        part_grad = grad_pre[s * tokens : (s + 1) * tokens]
        grads[s, 0:tokens, :] = part_grad
        edge_grad[8 * s : 8 * s + 8, :] = part_grad[0:8]
        for k in range(taps):
            first = 8 - reach + k
            conv_terms[k] = conv_terms[k] + jnp.sum(
                part_grad * padded[s, first : first + tokens, :], axis=0, keepdims=True
            )
    halo_back.start()
    pieces = [state_terms[i : i + 1] for i in range(2 * states)]
    pieces += conv_terms
    pieces.append(jnp.sum(grad_pre, axis=0, keepdims=True))
    pieces += [sums[0][i : i + 1] for i in range(states)]
    pieces += sums[1:]
    while len(pieces) < 2 * dp:
        pieces.append(jnp.zeros((1, width), F32))
    for i, piece in enumerate(pieces):
        small_part[i // 2, i % 2 : i % 2 + 1, :] = piece
    ex_small.start()
    small_slots[me] = small_part[me]

    def add_slots(refs):
        def add(k, total):
            return tuple(t + ref[k].astype(F32) for t, ref in zip(total, refs))

        return lax.fori_loop(0, dp, add, tuple(jnp.zeros(ref.shape[1:], F32) for ref in refs))

    ex_dtw.wait_recv()
    dtw_out[...] = unfold_lanes(add_slots((dtw_slots,))[0])
    halo_back.wait_recv()
    keep = jnp.where(me == dp - 1, 0.0, 1.0).astype(F32)
    for s in range(seqs):
        grads[s, tokens:, :] = after[8 * s : 8 * s + 8, :] * keep
        result = jnp.zeros((tokens, width), F32)
        for k in range(taps):
            late = reach - k
            result = result + conv_weight[k : k + 1, :] * grads[s, late : late + tokens, :]
        gradx_out[s] = result.astype(BF16)
    ex_small.wait_recv()
    small_all[me] = add_slots((small_slots,))[0]
    ex_total.start()
    ex_pw.wait_recv()
    proj_out[...] = unfold_lanes(add_slots((pw_slots,))[0])
    for ex in (ex_proj, ex_extra, ex_dt) + ex_one + ex_two + (ex_parts, ex_found, ex_dtw):
        ex.wait_send()
    halo.wait_send()
    halo_back.wait_send()
    ex_pw.wait_send()
    ex_small.wait_send()
    ex_total.wait_recv()
    ex_total.wait_send()


def output_body(
    states2, taps, gate, gradx, proj, dtw, small,
    gradx_out, gate_out, proj_out, state_out, dtw_out, weight_out, bias_out, dtb_out, alog_out, skip_out,
):
    gradx_out[...] = gradx[...]
    gate_out[...] = gate[...]
    proj_out[...] = proj[...]
    dtw_out[...] = dtw[...]
    states = states2 // 2
    targets = [(state_out, i) for i in range(states2)]
    targets += [(weight_out, i) for i in range(taps)]
    targets.append((bias_out, 0))
    targets += [(alog_out, i) for i in range(states)]
    targets += [(dtb_out, 0), (skip_out, 0)]
    for i, (target, row) in enumerate(targets):
        target[row : row + 1, :] = small[i // 2, i % 2 : i % 2 + 1, :]


def body(
    xin, zin, cotangent, conv_weight, conv_bias, proj_weight, dt_weight, dt_bias, a_log, d_skip
):
    dp = lax.axis_size("dp")
    expert = lax.axis_size("expert")
    seqs, tokens, width = xin.shape
    taps = conv_weight.shape[0]
    states = a_log.shape[0]
    rows = seqs * tokens
    part = dt_weight.shape[0]
    proj_rows = proj_weight.shape[0]
    rank = part * dp
    half = width // 2

    low_shape = (expert, rows // expert, rank)
    bc_shape = (expert, 2 * states // expert, rows)
    flat = (rows, width)
    cube = (seqs, tokens, width)
    fold = (2 * part, half)
    extra = (proj_rows - part, width)

    def f32(*shape):
        return pltpu.VMEM(shape, F32)

    def bf16(*shape):
        return pltpu.VMEM(shape, BF16)

    reduction = [bf16(*low_shape), f32(*bc_shape)] * 3
    scratch = [bf16(*fold), f32(*extra), bf16(*fold), bf16(8 * seqs, width)]
    scratch += [bf16(dp, *fold), f32(dp, *extra), bf16(dp, *fold), bf16(8 * seqs, width)]
    scratch += reduction + reduction
    scratch += [f32(dp, 3, width), f32(dp, 3, width), f32(dp, 2, width), f32(dp, 2, width)]
    scratch += [bf16(dp, *fold)] * 4 + [f32(dp, 2, width)] * 2 + [f32(8 * seqs, width)] * 2
    scratch += [f32(proj_rows * dp, width), bf16(proj_rows * dp, width), bf16(rank, width)]
    scratch += [f32(seqs, tokens + 8, width)] * 2
    scratch += [f32(*flat), bf16(*flat), f32(*flat), f32(*flat), f32(*flat), f32(*flat)]
    scratch += [f32(*flat)] * 4 + [f32(rows, CHUNK * states)] * 2
    scratch += [f32(rows, states, LANES)] * 2
    scratch += [f32(2 * states, rows), f32(2 * seqs, states, width)]
    scratch += [bf16(seqs, tokens + 1, states, width)] + [bf16(seqs, tokens, states, width)] * 2
    order = [dp] * 3 + [expert] * 8 + [dp] * 6
    for count in order:
        scratch += [pltpu.SemaphoreType.DMA((count,))] * 2
    scratch += [pltpu.SemaphoreType.DMA] * 4

    gate, gradx, proj, dtw, small = pl.pallas_call(
        functools.partial(core_body, dp, expert),
        out_shape=(
            sds(cube, BF16),
            sds(cube, BF16),
            sds((part, width), F32),
            sds((part, width), F32),
            sds((dp, 2, width), F32),
        ),
        in_specs=[whole] * 10,
        out_specs=(whole,) * 5,
        scratch_shapes=scratch,
        compiler_params=pltpu.CompilerParams(
            collective_id=1, has_side_effects=True, vmem_limit_bytes=VMEM_BYTES
        ),
        name="core",
    )(
        xin,
        zin,
        cotangent,
        conv_weight,
        conv_bias[None, :],
        proj_weight,
        dt_weight,
        dt_bias[None, :],
        a_log,
        d_skip[None, :],
    )
    row = sds((1, width), F32)
    results = pl.pallas_call(
        functools.partial(output_body, 2 * states, taps),
        out_shape=(
            sds(cube, BF16),
            sds(cube, BF16),
            sds((part, width), F32),
            sds((2 * states, width), F32),
            sds((part, width), F32),
            sds((taps, width), F32),
            row,
            row,
            sds((states, width), F32),
            row,
        ),
        in_specs=[whole] * 5,
        out_specs=(whole,) * 10,
        compiler_params=pltpu.CompilerParams(vmem_limit_bytes=VMEM_BYTES),
        name="outputs",
    )(gate, gradx, proj, dtw, small)
    results = list(results)
    for i in (6, 7, 9):
        results[i] = results[i].reshape(width)
    return tuple(results)


def solution(mesh):
    return jax.shard_map(
        body,
        mesh=mesh,
        in_specs=(
            P(None, "dp", "expert"),
            P(None, "dp", "expert"),
            P(None, "dp", "expert"),
            P(None, "expert"),
            P("expert"),
            P("dp", "expert"),
            P("dp", "expert"),
            P("expert"),
            P(None, "expert"),
            P("expert"),
        ),
        out_specs=(
            P(None, "dp", "expert"),
            P(None, "dp", "expert"),
            P("dp", "expert"),
            P(None, "expert"),
            P("dp", "expert"),
            P(None, "expert"),
            P("expert"),
            P("expert"),
            P(None, "expert"),
            P("expert"),
        ),
        check_vma=False,
    )
```

```python
import functools

import jax
import jax.numpy as jnp
from jax import lax
from jax.experimental import pallas as pl
from jax.experimental.pallas import tpu as pltpu
from jax.sharding import PartitionSpec as P

F32 = jnp.float32
BF16 = jnp.bfloat16
MESH = pl.DeviceIdType.MESH
LANES = 128
CHUNK = 16
VMEM_BYTES = 56 * 1024 * 1024

whole = pl.BlockSpec(memory_space=pltpu.VMEM)
sds = jax.ShapeDtypeStruct


def dot_nn(left, right, precision=None):
    return lax.dot_general(
        left, right, (((1,), (0,)), ((), ())), preferred_element_type=F32, precision=precision
    )


def dot_nt(left, right, precision=None):
    return lax.dot_general(
        left, right, (((1,), (1,)), ((), ())), preferred_element_type=F32, precision=precision
    )


def dot_tn(left, right):
    return lax.dot_general(left, right, (((0,), (0,)), ((), ())), preferred_element_type=F32)


def hail(axis, count, me):
    barrier = pltpu.get_barrier_semaphore()

    def one(k, carry):
        pl.semaphore_signal(
            barrier, inc=1, device_id={axis: lax.rem(me + k, count)}, device_id_type=MESH
        )
        return carry

    lax.fori_loop(1, count, one, 0)


def send_all(axis, count, me, source, landing, send_sem, recv_sem):
    def one(k, carry):
        peer = lax.rem(me + k, count)
        pltpu.make_async_remote_copy(
            src_ref=source(peer),
            dst_ref=landing(me),
            send_sem=send_sem.at[k],
            recv_sem=recv_sem.at[k],
            device_id={axis: peer},
            device_id_type=MESH,
        ).start()
        return carry

    lax.fori_loop(1, count, one, 0)


def wait_all(axis, count, me, source, landing, send_sem, recv_sem, sent):
    def one(k, carry):
        peer = lax.rem(me + k, count)
        origin = lax.rem(me + count - k, count)
        copy = pltpu.make_async_remote_copy(
            src_ref=source(peer),
            dst_ref=landing(origin),
            send_sem=send_sem.at[k],
            recv_sem=recv_sem.at[k],
            device_id={axis: peer},
            device_id_type=MESH,
        )
        if sent:
            copy.wait_send()
        else:
            copy.wait_recv()
        return carry

    lax.fori_loop(1, count, one, 0)


class Exchange:
    def __init__(self, axis, count, me, source, landing, sems):
        self.args = (axis, count, me, source, landing, sems[0], sems[1])

    def start(self):
        send_all(*self.args)

    def start_one(self, peer):
        axis, count, me, source, landing, send_sem, recv_sem = self.args
        k = lax.rem(peer - me + count, count)
        pltpu.make_async_remote_copy(
            src_ref=source(peer),
            dst_ref=landing(me),
            send_sem=send_sem.at[k],
            recv_sem=recv_sem.at[k],
            device_id={axis: peer},
            device_id_type=MESH,
        ).start()

    def wait_recv(self):
        wait_all(*self.args, False)

    def wait_send(self):
        wait_all(*self.args, True)


def fold_lanes(value):
    half = value.shape[1] // 2
    return jnp.concatenate([value[:, :half], value[:, half:]], 0)


def unfold_lanes(value):
    half = value.shape[0] // 2
    return jnp.concatenate([value[:half], value[half:]], 1)


def views(refs, first, count, lanes):
    first = pl.multiple_of(first, count)
    return [ref.at[pl.ds(first, count), lanes] for ref in refs]


def reduce_start(ex_low, ex_bc, low_slots, bc_slots, low, bc, me):
    ex_low.start()
    ex_bc.start()
    low_slots[me] = low[me]
    bc_slots[me] = bc[me]


def reduce_middle(ex, low_slots, bc_slots, low_all, bc_all, me, count):
    ex[0].wait_recv()
    ex[1].wait_recv()

    def add(k, total):
        return (total[0] + low_slots[k].astype(F32), total[1] + bc_slots[k])

    zero = (jnp.zeros(low_slots.shape[1:], F32), jnp.zeros(bc_slots.shape[1:], F32))
    low_sum, bc_sum = lax.fori_loop(0, count, add, zero)
    low_all[me] = low_sum.astype(BF16)
    bc_all[me] = bc_sum
    ex[2].start()
    ex[3].start()


def spread_rows(source, target):
    per = source.shape[1]
    for e in range(source.shape[0]):
        target[e * per : (e + 1) * per, :] = source[e]


def core_body(
    dp, expert,
    xin, zin, cot, conv_weight, conv_bias, proj_mine, dt_mine, dt_bias, a_log, d_skip,
    gate_out, gradx_out, proj_out, dtw_out, small_all,
    send_proj, send_extra, send_dt, send_edge, all_proj, all_extra, all_dt, front,
    low_part, bc_part, low_slots, bc_slots, low_all, bc_all,
    part2, slots2, all2,
    parts, slots, found, incoming,
    dtw_part, dtw_slots, pw_part, pw_slots, small_part, small_slots, edge_grad, after,
    proj_wide, proj_full, dt_full, padded, grads, preact, xconv, pre, step, gy, gate_factor,
    u_rows, y_rows, b_rows, g_rows, u_half, gy_half, g_half, b_diag, c_diag,
    bx, cx, bc_rows, begin, hist, adjoint, prevs, decays, b_in, c_in,
    *sems,
):
    seqs, tokens, width = zin.shape
    states = a_log.shape[0]
    taps = conv_weight.shape[0]
    reach = taps - 1
    rows = seqs * tokens
    rank = dt_full.shape[0]
    part = dt_mine.shape[0]
    proj_rows = proj_mine.shape[0]
    me = lax.axis_index("dp")
    mine = lax.axis_index("expert")
    hail("dp", dp, me)
    hail("expert", expert, mine)

    pairs = iter(range(0, len(sems), 2))

    def next_pair():
        i = next(pairs)
        return (sems[i], sems[i + 1])

    def over_dp(source, landing):
        return Exchange("dp", dp, me, source, landing, next_pair())

    def over_expert(source, landing):
        return Exchange("expert", expert, mine, source, landing, next_pair())

    def reduction(low, bc, low_in, bc_in, low_out, bc_out):
        return (
            over_expert(lambda p: low.at[p], lambda d: low_in.at[d]),
            over_expert(lambda p: bc.at[p], lambda d: bc_in.at[d]),
            over_expert(lambda p: low_out.at[mine], lambda d: low_out.at[d]),
            over_expert(lambda p: bc_out.at[mine], lambda d: bc_out.at[d]),
        )

    ex_proj = over_dp(lambda p: send_proj, lambda d: all_proj.at[d])
    ex_extra = over_dp(lambda p: send_extra, lambda d: all_extra.at[d])
    ex_dt = over_dp(lambda p: send_dt, lambda d: all_dt.at[d])
    ex_one = reduction(low_part, bc_part, low_slots, bc_slots, low_all, bc_all)
    ex_two = over_expert(lambda p: part2.at[p], lambda d: slots2.at[d])
    ex_three = over_expert(lambda p: all2.at[mine], lambda d: all2.at[d])
    ex_parts = over_dp(lambda p: parts.at[p], lambda d: slots.at[d])
    ex_found = over_dp(lambda p: found.at[p], lambda d: incoming.at[d])
    ex_dtw = over_dp(lambda p: dtw_part.at[p], lambda d: dtw_slots.at[d])
    ex_pw = over_dp(lambda p: pw_part.at[p], lambda d: pw_slots.at[d])
    ex_small = over_dp(lambda p: small_part.at[p], lambda d: small_slots.at[d])
    ex_total = over_dp(lambda p: small_all.at[me], lambda d: small_all.at[d])

    def neighbour(source, target, distance):
        pair = next_pair()
        return pltpu.make_async_remote_copy(
            src_ref=source,
            dst_ref=target,
            send_sem=pair[0],
            recv_sem=pair[1],
            device_id={"dp": lax.rem(me + dp + distance, dp)},
            device_id_type=MESH,
        )

    halo = neighbour(send_edge, front, 1)
    halo_back = neighbour(edge_grad, after, -1)

    proj32 = proj_mine[...].astype(F32)
    send_proj[...] = fold_lanes(proj32[:part]).astype(BF16)
    send_extra[...] = proj32[part:]
    send_dt[...] = fold_lanes(dt_mine[...].astype(F32)).astype(BF16)
    send_edge[...] = jnp.concatenate(
        [xin[s, tokens - 16 :, :].astype(F32)[8:] for s in range(seqs)], 0
    ).astype(BF16)
    all_proj[me] = send_proj[...]
    all_extra[me] = send_extra[...]
    all_dt[me] = send_dt[...]
    for s in range(seqs):
        here = slice(s * tokens, (s + 1) * tokens)
        z = zin[s].astype(F32)
        g = cot[s].astype(F32)
        sig = lax.logistic(z)
        gy[here, :] = g * z * sig
        gate_factor[here, :] = g * sig * (1.0 + z * (1.0 - sig))
        padded[s, 8:, :] = xin[s].astype(F32)
    rate_all = -jnp.exp(a_log[...])
    pl.semaphore_wait(pltpu.get_barrier_semaphore(), dp + expert - 2)

    halo.start()
    ex_proj.start()
    ex_extra.start()
    ex_dt.start()

    halo.wait_recv()
    keep = jnp.where(me == 0, 0.0, 1.0).astype(F32)
    lead = front[...].astype(F32) * keep
    for s in range(seqs):
        padded[s, 8 - reach : 8, :] = lead[8 * s + 8 - reach : 8 * s + 8, :]
        value = conv_bias[...] + jnp.zeros((tokens, width), F32)
        for k in range(taps):
            first = 8 - reach + k
            value = value + conv_weight[k : k + 1, :] * padded[s, first : first + tokens, :]
        here = slice(s * tokens, (s + 1) * tokens)
        preact[here, :] = value
        xconv[here, :] = (value * lax.logistic(value)).astype(BF16)
    ex_proj.wait_recv()
    ex_extra.wait_recv()
    for i in range(dp):
        proj_wide[i * proj_rows : i * proj_rows + part, :] = unfold_lanes(all_proj[i].astype(F32))
        proj_wide[i * proj_rows + part : (i + 1) * proj_rows, :] = all_extra[i]
    total = rank + 2 * states
    proj_full[0:total, :] = proj_wide[...].astype(BF16)
    proj_full[total:, :] = jnp.zeros((proj_full.shape[0] - total, width), BF16)
    x_flat = xconv[...]
    bc = dot_nt(proj_full[rank:total, :], x_flat)
    per = bc_part.shape[1]
    for e in range(expert):
        bc_part[e] = bc[e * per : (e + 1) * per, :]
    low_part[...] = dot_nt(x_flat, proj_full[0:rank, :]).reshape(low_part.shape).astype(BF16)
    reduce_start(ex_one[0], ex_one[1], low_slots, bc_slots, low_part, bc_part, mine)
    ex_dt.wait_recv()
    for i in range(0, dp, 2):
        pair = [unfold_lanes(all_dt[i + j].astype(F32)) for j in range(2)]
        dt_full[i * part : (i + 2) * part, :] = jnp.concatenate(pair, 0).astype(BF16)
    reduce_middle(ex_one, low_slots, bc_slots, low_all, bc_all, mine, expert)
    ex_one[3].wait_recv()
    spread_rows(bc_all, bc_rows)
    for r in range(rows):
        bx[r] = jnp.broadcast_to(bc_rows[0:states, r : r + 1], (states, LANES))
        cx[r] = jnp.broadcast_to(bc_rows[states : 2 * states, r : r + 1], (states, LANES))
    ex_one[2].wait_recv()
    low = low_all[...].reshape(rows, rank)
    pre_value = dot_nn(low, dt_full[...]) + dt_bias[...]
    pre[...] = pre_value
    step_value = jnp.maximum(pre_value, 0.0) + jnp.log1p(jnp.exp(-jnp.abs(pre_value)))
    step[...] = step_value
    u_rows[...] = step_value * xconv[...].astype(F32)

    wide = 2 * LANES

    def across_lanes(tile, count):
        return jnp.concatenate([tile] * count, 1)

    for block in range(width // wide):
        lanes = slice(block * wide, (block + 1) * wide)
        rate = rate_all[:, lanes]

        def alone(k, carried):
            ahead = list(carried[:seqs])
            behind = list(carried[seqs:])
            for s in range(seqs):
                first = s * tokens + k * 8
                last = s * tokens + tokens - (k + 1) * 8
                step_f, u_f = views((step, u_rows), first, 8, lanes)
                step_b, gy_b = views((step, gy), last, 8, lanes)
                for i in range(8):
                    now = jnp.exp(step_f[i : i + 1, :] * rate)
                    b_tile = across_lanes(bx[first + i], 2)
                    ahead[s] = now * ahead[s] + b_tile * u_f[i : i + 1, :]
                    j = 7 - i
                    now = jnp.exp(step_b[j : j + 1, :] * rate)
                    c_tile = across_lanes(cx[last + j], 2)
                    behind[s] = now * (c_tile * gy_b[j : j + 1, :] + behind[s])
            return tuple(ahead + behind)

        zero = jnp.zeros((states, wide), F32)
        ends = lax.fori_loop(0, tokens // 8, alone, (zero,) * (2 * seqs))
        for s in range(seqs):
            total = jnp.sum(step[s * tokens : (s + 1) * tokens, lanes], axis=0, keepdims=True)
            passing = jnp.exp(rate * total)
            for n in range(states):
                parts[s * states + n, 0:1, lanes] = ends[s][n : n + 1, :]
                parts[s * states + n, 1:2, lanes] = ends[seqs + s][n : n + 1, :]
                parts[s * states + n, 2:3, lanes] = passing[n : n + 1, :]

    ex_parts.start()
    slots[me] = parts[me]
    span = CHUNK * states
    turns = tokens // CHUNK
    spread = (
        (lax.broadcasted_iota(jnp.int32, (states, span), 1) & (states - 1))
        == lax.broadcasted_iota(jnp.int32, (states, span), 0)
    ).astype(F32)
    spread_half = spread.astype(BF16)
    own = (
        lax.shift_right_logical(
            lax.broadcasted_iota(jnp.int32, (rows, span), 1), states.bit_length() - 1
        )
        == (lax.broadcasted_iota(jnp.int32, (rows, span), 0) & (CHUNK - 1))
    ).astype(F32)
    across = jnp.transpose(bc_rows[...])
    b_diag[...] = (dot_nn(across[:, :states].astype(BF16), spread_half) * own).astype(BF16)
    c_diag[...] = (dot_nn(across[:, states:].astype(BF16), spread_half) * own).astype(BF16)
    own = own[:CHUNK]
    fold = own.astype(BF16)
    lanes_row = lax.broadcasted_iota(jnp.int32, (LANES, 2 * span), 0)
    lanes_col = lax.broadcasted_iota(jnp.int32, (LANES, 2 * span), 1)
    target = (lanes_col & (states - 1)) + jnp.where(lanes_col < span, 0, states)
    gather_bc = (lanes_row == target).astype(F32).astype(BF16)
    u_half[...] = u_rows[...].astype(BF16)
    gy_half[...] = gy[...].astype(BF16)

    def prepare(k, carry):
        step_v, u_v = views((step, u_rows), k * 8, 8, slice(0, width))
        for i in range(8):
            r = k * 8 + i
            decays[r] = jnp.exp(step_v[i : i + 1, :] * rate_all)
            b_in[r] = across_lanes(bx[r], width // LANES) * u_v[i : i + 1, :]
        return carry

    lax.fori_loop(0, rows // 8, prepare, 0)
    ex_parts.wait_recv()

    def prefix(k, carried):
        ahead, behind = carried
        late = dp - 1 - k
        found[k, 0:1, :] = ahead
        found[late, 1:2, :] = behind
        ahead = slots[k, 2:3, :] * ahead + slots[k, 0:1, :]
        behind = slots[late, 2:3, :] * behind + slots[late, 1:2, :]
        return (ahead, behind)

    zero = jnp.zeros((1, width), F32)
    lax.fori_loop(0, dp, prefix, (zero, zero))
    ex_found.start()
    incoming[me] = found[me]

    def prepare_back(k, carry):
        gy_v = views((gy,), k * 8, 8, slice(0, width))[0]
        for i in range(8):
            r = k * 8 + i
            c_in[r] = across_lanes(cx[r], width // LANES) * gy_v[i : i + 1, :]
        return carry

    lax.fori_loop(0, rows // 8, prepare_back, 0)
    ex_found.wait_recv()
    for s in range(seqs):
        for n in range(states):
            begin[s, n : n + 1, :] = incoming[s * states + n, 0:1, :]
            begin[seqs + s, n : n + 1, :] = incoming[s * states + n, 1:2, :]
        hist[s, 0] = begin[s].astype(BF16)

    def forward(k, carried):
        carried = list(carried)
        for s in range(seqs):
            for i in range(8):
                t = k * 8 + i
                carried[s] = decays[s * tokens + t] * carried[s] + b_in[s * tokens + t]
                hist[s, t + 1] = carried[s].astype(BF16)
        return tuple(carried)

    lax.fori_loop(0, tokens // 8, forward, tuple(begin[s] for s in range(seqs)))

    def backward(k, carried):
        passed = list(carried[:seqs])
        rate_grad = carried[seqs]
        chunk = turns - 1 - k
        first = chunk * CHUNK
        folded = []
        rounded = []
        for s in range(seqs):
            here = pl.ds(pl.multiple_of(s * tokens + first, CHUNK), CHUNK)
            step_v = step.at[here, :]
            for i in reversed(range(CHUNK)):
                r = s * tokens + first + i
                adj = c_in[r] + passed[s]
                adjoint[s, i] = adj.astype(BF16)
                passed[s] = decays[r] * adj
                prev = passed[s] * hist[s, first + i].astype(F32) * rate_all
                prevs[s, i] = prev.astype(BF16)
                rate_grad = rate_grad + prev * step_v[i : i + 1, :]
            history = hist[s, pl.ds(first + 1, CHUNK)].reshape(span, width)
            adj = adjoint[s].reshape(span, width)
            b_adjoint = dot_nn(b_diag[here, :], adj)
            summed = dot_nn(fold, prevs[s].reshape(span, width))
            grad_b = dot_nt(u_half[here, :], adj) * own
            grad_c = dot_nt(gy_half[here, :], history) * own
            folded.append(jnp.concatenate([grad_b, grad_c], 1))
            x = xconv[here, :].astype(F32)
            grad_pre = (x * b_adjoint + summed) * lax.logistic(pre[here, :])
            g_rows[here, :] = grad_pre
            rounded.append(grad_pre.astype(BF16))
            g_half[here, :] = rounded[s]
            b_rows[here, :] = d_skip[...] * gy[here, :] + step[here, :] * b_adjoint
        folded = jnp.concatenate(folded, 0)
        coarse = folded.astype(BF16)
        fine = (folded - coarse.astype(F32)).astype(BF16)
        halves = dot_nt(jnp.concatenate([coarse, fine], 0), gather_bc)
        grad_bc = halves[: seqs * CHUNK] + halves[seqs * CHUNK :]
        low_grad = dot_nt(jnp.concatenate(rounded, 0), dt_full[...])
        message = jnp.concatenate([low_grad, grad_bc], 1).astype(BF16)
        for s in range(seqs):
            owner = s * turns + chunk
            part2[owner] = message[s * CHUNK : (s + 1) * CHUNK]

            @pl.when(mine != owner)
            def _():
                ex_two.start_one(owner)

            @pl.when(mine == owner)
            def _():
                slots2[mine] = part2[mine]

        return tuple(passed) + (rate_grad,)

    ends = lax.fori_loop(
        0,
        turns,
        backward,
        tuple(begin[seqs + s] for s in range(seqs)) + (jnp.zeros((states, width), F32),),
    )
    rate_sum = ends[seqs]

    dtw = dot_tn(low_all[...].reshape(rows, rank), g_half[...])
    for i in range(dp):
        dtw_part[i] = fold_lanes(dtw[i * part : (i + 1) * part]).astype(BF16)
    ex_dtw.start()
    dtw_slots[me] = dtw_part[me]
    x = xconv[...].astype(F32)
    sums = [rate_sum]
    sums.append(jnp.sum(g_rows[...], axis=0, keepdims=True))
    sums.append(jnp.sum(gy[...] * x, axis=0, keepdims=True))
    ex_two.wait_recv()

    def add_messages(k, total):
        return total + slots2[k].astype(F32)

    zero = jnp.zeros(slots2.shape[1:], F32)
    all2[mine] = lax.fori_loop(0, expert, add_messages, zero).astype(BF16)
    ex_three.start()
    for s in range(seqs):
        for k in range(turns):
            t = k * CHUNK
            here = slice(s * tokens + t, s * tokens + t + CHUNK)
            history = hist[s, t + 1 : t + 1 + CHUNK].reshape(span, width)
            y_rows[here, :] = dot_nn(c_diag[here, :], history)
    y_value = y_rows[...] + d_skip[...] * x
    gate_out[...] = (y_value * gate_factor[...]).astype(BF16).reshape(gate_out.shape)
    ex_three.wait_recv()

    grad_projected = all2[...].reshape(rows, all2.shape[2])
    x_flat = xconv[...]
    grad_conv = b_rows[...] + dot_nn(grad_projected, proj_full[...])
    state_terms = dot_tn(grad_projected[:, rank:], x_flat)
    value = preact[...]
    sig = lax.logistic(value)
    grad_pre = grad_conv * sig * (1.0 + value * (1.0 - sig))
    conv_terms = [jnp.zeros((1, width), F32) for k in range(taps)]
    for s in range(seqs):
        part_grad = grad_pre[s * tokens : (s + 1) * tokens]
        grads[s, 0:tokens, :] = part_grad
        edge_grad[8 * s : 8 * s + 8, :] = part_grad[0:8]
        for k in range(taps):
            first = 8 - reach + k
            conv_terms[k] = conv_terms[k] + jnp.sum(
                part_grad * padded[s, first : first + tokens, :], axis=0, keepdims=True
            )
    halo_back.start()
    pieces = [state_terms[i : i + 1] for i in range(2 * states)]
    pieces += conv_terms
    pieces.append(jnp.sum(grad_pre, axis=0, keepdims=True))
    pieces += [sums[0][i : i + 1] for i in range(states)]
    pieces += sums[1:]
    while len(pieces) < 2 * dp:
        pieces.append(jnp.zeros((1, width), F32))
    for i, piece in enumerate(pieces):
        small_part[i // 2, i % 2 : i % 2 + 1, :] = piece
    ex_small.start()
    small_slots[me] = small_part[me]
    pw = dot_tn(grad_projected[:, :rank], x_flat)
    for i in range(dp):
        pw_part[i] = fold_lanes(pw[i * part : (i + 1) * part]).astype(BF16)
    ex_pw.start()
    pw_slots[me] = pw_part[me]

    def add_slots(refs):
        def add(k, total):
            return tuple(t + ref[k].astype(F32) for t, ref in zip(total, refs))

        return lax.fori_loop(0, dp, add, tuple(jnp.zeros(ref.shape[1:], F32) for ref in refs))

    ex_dtw.wait_recv()
    dtw_out[...] = unfold_lanes(add_slots((dtw_slots,))[0])
    halo_back.wait_recv()
    keep = jnp.where(me == dp - 1, 0.0, 1.0).astype(F32)
    for s in range(seqs):
        grads[s, tokens:, :] = after[8 * s : 8 * s + 8, :] * keep
        result = jnp.zeros((tokens, width), F32)
        for k in range(taps):
            late = reach - k
            result = result + conv_weight[k : k + 1, :] * grads[s, late : late + tokens, :]
        gradx_out[s] = result.astype(BF16)
    ex_small.wait_recv()
    small_all[me] = add_slots((small_slots,))[0]
    ex_total.start()
    ex_pw.wait_recv()
    proj_out[...] = unfold_lanes(add_slots((pw_slots,))[0])
    for ex in (ex_proj, ex_extra, ex_dt) + ex_one + (ex_two, ex_three, ex_parts, ex_found, ex_dtw):
        ex.wait_send()
    halo.wait_send()
    halo_back.wait_send()
    ex_pw.wait_send()
    ex_small.wait_send()
    ex_total.wait_recv()
    ex_total.wait_send()


def output_body(
    states2, taps, gate, gradx, proj, dtw, small,
    gradx_out, gate_out, proj_out, state_out, dtw_out, weight_out, bias_out, dtb_out, alog_out, skip_out,
):
    gradx_out[...] = gradx[...]
    gate_out[...] = gate[...]
    proj_out[...] = proj[...]
    dtw_out[...] = dtw[...]
    states = states2 // 2
    targets = [(state_out, i) for i in range(states2)]
    targets += [(weight_out, i) for i in range(taps)]
    targets.append((bias_out, 0))
    targets += [(alog_out, i) for i in range(states)]
    targets += [(dtb_out, 0), (skip_out, 0)]
    for i, (target, row) in enumerate(targets):
        target[row : row + 1, :] = small[i // 2, i % 2 : i % 2 + 1, :]


def body(
    xin, zin, cotangent, conv_weight, conv_bias, proj_weight, dt_weight, dt_bias, a_log, d_skip
):
    dp = lax.axis_size("dp")
    expert = lax.axis_size("expert")
    seqs, tokens, width = xin.shape
    taps = conv_weight.shape[0]
    states = a_log.shape[0]
    rows = seqs * tokens
    part = dt_weight.shape[0]
    proj_rows = proj_weight.shape[0]
    rank = part * dp
    half = width // 2

    low_shape = (expert, rows // expert, rank)
    bc_shape = (expert, 2 * states // expert, rows)
    flat = (rows, width)
    cube = (seqs, tokens, width)
    fold = (2 * part, half)
    extra = (proj_rows - part, width)

    def f32(*shape):
        return pltpu.VMEM(shape, F32)

    def bf16(*shape):
        return pltpu.VMEM(shape, BF16)

    reduction = [bf16(*low_shape), f32(*bc_shape)] * 3
    scratch = [bf16(*fold), f32(*extra), bf16(*fold), bf16(8 * seqs, width)]
    scratch += [bf16(dp, *fold), f32(dp, *extra), bf16(dp, *fold), bf16(8 * seqs, width)]
    scratch += reduction + [bf16(expert, rows // expert, rank + LANES)] * 3
    scratch += [f32(dp, 3, width), f32(dp, 3, width), f32(dp, 2, width), f32(dp, 2, width)]
    scratch += [bf16(dp, *fold)] * 4 + [f32(dp, 2, width)] * 2 + [f32(8 * seqs, width)] * 2
    scratch += [f32(proj_rows * dp, width), bf16(rank + LANES, width), bf16(rank, width)]
    scratch += [f32(seqs, tokens + 8, width)] * 2
    scratch += [f32(*flat), bf16(*flat), f32(*flat), f32(*flat), f32(*flat), f32(*flat)]
    scratch += [f32(*flat)] * 4 + [bf16(*flat)] * 3 + [bf16(rows, CHUNK * states)] * 2
    scratch += [f32(rows, states, LANES)] * 2
    scratch += [f32(2 * states, rows), f32(2 * seqs, states, width)]
    scratch += [bf16(seqs, tokens + 1, states, width)] + [bf16(seqs, CHUNK, states, width)] * 2
    scratch += [f32(rows, states, width)] * 3
    order = [dp] * 3 + [expert] * 6 + [dp] * 6
    for count in order:
        scratch += [pltpu.SemaphoreType.DMA((count,))] * 2
    scratch += [pltpu.SemaphoreType.DMA] * 4

    gate, gradx, proj, dtw, small = pl.pallas_call(
        functools.partial(core_body, dp, expert),
        out_shape=(
            sds(cube, BF16),
            sds(cube, BF16),
            sds((part, width), F32),
            sds((part, width), F32),
            sds((dp, 2, width), F32),
        ),
        in_specs=[whole] * 10,
        out_specs=(whole,) * 5,
        scratch_shapes=scratch,
        compiler_params=pltpu.CompilerParams(
            collective_id=1, has_side_effects=True, vmem_limit_bytes=VMEM_BYTES
        ),
        name="core",
    )(
        xin,
        zin,
        cotangent,
        conv_weight,
        conv_bias[None, :],
        proj_weight,
        dt_weight,
        dt_bias[None, :],
        a_log,
        d_skip[None, :],
    )
    row = sds((1, width), F32)
    results = pl.pallas_call(
        functools.partial(output_body, 2 * states, taps),
        out_shape=(
            sds(cube, BF16),
            sds(cube, BF16),
            sds((part, width), F32),
            sds((2 * states, width), F32),
            sds((part, width), F32),
            sds((taps, width), F32),
            row,
            row,
            sds((states, width), F32),
            row,
        ),
        in_specs=[whole] * 5,
        out_specs=(whole,) * 10,
        compiler_params=pltpu.CompilerParams(vmem_limit_bytes=VMEM_BYTES),
        name="outputs",
    )(gate, gradx, proj, dtw, small)
    results = list(results)
    for i in (6, 7, 9):
        results[i] = results[i].reshape(width)
    return tuple(results)


def solution(mesh):
    return jax.shard_map(
        body,
        mesh=mesh,
        in_specs=(
            P(None, "dp", "expert"),
            P(None, "dp", "expert"),
            P(None, "dp", "expert"),
            P(None, "expert"),
            P("expert"),
            P("dp", "expert"),
            P("dp", "expert"),
            P("expert"),
            P(None, "expert"),
            P("expert"),
        ),
        out_specs=(
            P(None, "dp", "expert"),
            P(None, "dp", "expert"),
            P("dp", "expert"),
            P(None, "expert"),
            P("dp", "expert"),
            P(None, "expert"),
            P("expert"),
            P("expert"),
            P(None, "expert"),
            P("expert"),
        ),
        check_vma=False,
    )
```

```python
import functools

import jax
import jax.numpy as jnp
from jax import lax
from jax.experimental import pallas as pl
from jax.experimental.pallas import tpu as pltpu
from jax.sharding import PartitionSpec as P

F32 = jnp.float32
BF16 = jnp.bfloat16
MESH = pl.DeviceIdType.MESH
LANES = 128
CHUNK = 16
VMEM_BYTES = 56 * 1024 * 1024

whole = pl.BlockSpec(memory_space=pltpu.VMEM)
sds = jax.ShapeDtypeStruct


def dot_nn(left, right, precision=None):
    return lax.dot_general(
        left, right, (((1,), (0,)), ((), ())), preferred_element_type=F32, precision=precision
    )


def dot_nt(left, right, precision=None):
    return lax.dot_general(
        left, right, (((1,), (1,)), ((), ())), preferred_element_type=F32, precision=precision
    )


def dot_tn(left, right):
    return lax.dot_general(left, right, (((0,), (0,)), ((), ())), preferred_element_type=F32)


def hail(axis, count, me):
    barrier = pltpu.get_barrier_semaphore()
    for k in range(1, count):
        pl.semaphore_signal(
            barrier, inc=1, device_id={axis: lax.rem(me + k, count)}, device_id_type=MESH
        )


class Exchange:
    def __init__(self, axis, count, me, source, landing, sems):
        self.axis, self.count, self.me = axis, count, me
        self.source, self.landing = source, landing
        self.send_sem, self.recv_sem = sems

    def start_one(self, peer):
        pltpu.make_async_remote_copy(
            src_ref=self.source(peer),
            dst_ref=self.landing.at[self.me],
            send_sem=self.send_sem,
            recv_sem=self.recv_sem,
            device_id={self.axis: peer},
            device_id_type=MESH,
        ).start()

    def start(self):
        for k in range(1, self.count):
            self.start_one(lax.rem(self.me + k, self.count))

    def wait_bytes(self, sem):
        others = self.landing.at[pl.ds(0, self.count - 1)]
        pltpu.make_async_copy(others, others, sem).wait()

    def wait_recv(self):
        self.wait_bytes(self.recv_sem)

    def wait_send(self):
        self.wait_bytes(self.send_sem)


def fold_lanes(value):
    half = value.shape[1] // 2
    return jnp.concatenate([value[:, :half], value[:, half:]], 0)


def unfold_lanes(value):
    half = value.shape[0] // 2
    return jnp.concatenate([value[:half], value[half:]], 1)


def views(refs, first, count, lanes):
    first = pl.multiple_of(first, count)
    return [ref.at[pl.ds(first, count), lanes] for ref in refs]


def reduce_start(ex_low, ex_bc, low_slots, bc_slots, low, bc, me):
    ex_low.start()
    ex_bc.start()
    low_slots[me] = low[me]
    bc_slots[me] = bc[me]


def reduce_middle(ex, low_slots, bc_slots, low_all, bc_all, me, count):
    ex[0].wait_recv()
    ex[1].wait_recv()

    def add(k, total):
        return (total[0] + low_slots[k].astype(F32), total[1] + bc_slots[k])

    zero = (jnp.zeros(low_slots.shape[1:], F32), jnp.zeros(bc_slots.shape[1:], F32))
    low_sum, bc_sum = lax.fori_loop(0, count, add, zero)
    low_all[me] = low_sum.astype(BF16)
    bc_all[me] = bc_sum
    ex[2].start()
    ex[3].start()


def spread_rows(source, target):
    per = source.shape[1]
    for e in range(source.shape[0]):
        target[e * per : (e + 1) * per, :] = source[e]


def core_body(
    dp, expert,
    xin, zin, cot, conv_weight, conv_bias, proj_mine, dt_mine, dt_bias, a_log, d_skip,
    gate_out, gradx_out, proj_out, dtw_out, small_all,
    send_proj, send_extra, send_dt, send_edge, all_proj, all_extra, all_dt, front,
    low_part, bc_part, low_slots, bc_slots, low_all, bc_all,
    part2, slots2, all2,
    parts, slots, found, incoming,
    dtw_part, dtw_slots, pw_part, pw_slots, small_part, small_slots, edge_grad, after,
    proj_wide, proj_full, dt_full, padded, grads, preact, xconv, pre, step, gy, gate_factor,
    u_rows, y_rows, b_rows, g_rows, u_half, gy_half, g_half, b_diag, c_diag,
    bx, cx, bc_rows, begin, hist, adjoint, prevs, decays, b_in, c_in,
    *sems,
):
    seqs, tokens, width = zin.shape
    states = a_log.shape[0]
    taps = conv_weight.shape[0]
    reach = taps - 1
    rows = seqs * tokens
    rank = dt_full.shape[0]
    part = dt_mine.shape[0]
    proj_rows = proj_mine.shape[0]
    me = lax.axis_index("dp")
    mine = lax.axis_index("expert")
    hail("dp", dp, me)
    hail("expert", expert, mine)

    pairs = iter(range(0, len(sems), 2))

    def next_pair():
        i = next(pairs)
        return (sems[i], sems[i + 1])

    def over_dp(source, landing):
        return Exchange("dp", dp, me, source, landing, next_pair())

    def over_expert(source, landing):
        return Exchange("expert", expert, mine, source, landing, next_pair())

    def reduction(low, bc, low_in, bc_in, low_out, bc_out):
        return (
            over_expert(lambda p: low.at[p], low_in),
            over_expert(lambda p: bc.at[p], bc_in),
            over_expert(lambda p: low_out.at[mine], low_out),
            over_expert(lambda p: bc_out.at[mine], bc_out),
        )

    ex_proj = over_dp(lambda p: send_proj, all_proj)
    ex_extra = over_dp(lambda p: send_extra, all_extra)
    ex_dt = over_dp(lambda p: send_dt, all_dt)
    ex_one = reduction(low_part, bc_part, low_slots, bc_slots, low_all, bc_all)
    ex_two = over_expert(lambda p: part2.at[p], slots2)
    ex_three = over_expert(lambda p: all2.at[mine], all2)
    ex_parts = over_dp(lambda p: parts.at[p], slots)
    ex_found = over_dp(lambda p: found.at[p], incoming)
    ex_dtw = over_dp(lambda p: dtw_part.at[p], dtw_slots)
    ex_pw = over_dp(lambda p: pw_part.at[p], pw_slots)
    ex_small = over_dp(lambda p: small_part.at[p], small_slots)
    ex_total = over_dp(lambda p: small_all.at[me], small_all)

    def neighbour(source, target, distance):
        pair = next_pair()
        return pltpu.make_async_remote_copy(
            src_ref=source,
            dst_ref=target,
            send_sem=pair[0],
            recv_sem=pair[1],
            device_id={"dp": lax.rem(me + dp + distance, dp)},
            device_id_type=MESH,
        )

    halo = neighbour(send_edge, front, 1)
    halo_back = neighbour(edge_grad, after, -1)

    proj32 = proj_mine[...].astype(F32)
    send_proj[...] = fold_lanes(proj32[:part]).astype(BF16)
    send_extra[...] = proj32[part:]
    send_dt[...] = fold_lanes(dt_mine[...].astype(F32)).astype(BF16)
    send_edge[...] = jnp.concatenate(
        [xin[s, tokens - 16 :, :].astype(F32)[8:] for s in range(seqs)], 0
    ).astype(BF16)
    all_proj[me] = send_proj[...]
    all_extra[me] = send_extra[...]
    all_dt[me] = send_dt[...]
    for s in range(seqs):
        here = slice(s * tokens, (s + 1) * tokens)
        z = zin[s].astype(F32)
        g = cot[s].astype(F32)
        sig = lax.logistic(z)
        gy[here, :] = g * z * sig
        gate_factor[here, :] = g * sig * (1.0 + z * (1.0 - sig))
        padded[s, 8:, :] = xin[s].astype(F32)
    rate_all = -jnp.exp(a_log[...])
    pl.semaphore_wait(pltpu.get_barrier_semaphore(), dp + expert - 2)

    halo.start()
    ex_proj.start()
    ex_extra.start()
    ex_dt.start()

    halo.wait_recv()
    keep = jnp.where(me == 0, 0.0, 1.0).astype(F32)
    lead = front[...].astype(F32) * keep
    for s in range(seqs):
        padded[s, 8 - reach : 8, :] = lead[8 * s + 8 - reach : 8 * s + 8, :]
        value = conv_bias[...] + jnp.zeros((tokens, width), F32)
        for k in range(taps):
            first = 8 - reach + k
            value = value + conv_weight[k : k + 1, :] * padded[s, first : first + tokens, :]
        here = slice(s * tokens, (s + 1) * tokens)
        preact[here, :] = value
        xconv[here, :] = (value * lax.logistic(value)).astype(BF16)
    ex_proj.wait_recv()
    ex_extra.wait_recv()
    for i in range(dp):
        proj_wide[i * proj_rows : i * proj_rows + part, :] = unfold_lanes(all_proj[i].astype(F32))
        proj_wide[i * proj_rows + part : (i + 1) * proj_rows, :] = all_extra[i]
    total = rank + 2 * states
    proj_full[0:total, :] = proj_wide[...].astype(BF16)
    proj_full[total:, :] = jnp.zeros((proj_full.shape[0] - total, width), BF16)
    x_flat = xconv[...]
    bc = dot_nt(proj_full[rank:total, :], x_flat)
    per = bc_part.shape[1]
    for e in range(expert):
        bc_part[e] = bc[e * per : (e + 1) * per, :]
    low_part[...] = dot_nt(x_flat, proj_full[0:rank, :]).reshape(low_part.shape).astype(BF16)
    reduce_start(ex_one[0], ex_one[1], low_slots, bc_slots, low_part, bc_part, mine)
    ex_dt.wait_recv()
    for i in range(0, dp, 2):
        pair = [unfold_lanes(all_dt[i + j].astype(F32)) for j in range(2)]
        dt_full[i * part : (i + 2) * part, :] = jnp.concatenate(pair, 0).astype(BF16)
    reduce_middle(ex_one, low_slots, bc_slots, low_all, bc_all, mine, expert)
    ex_one[3].wait_recv()
    spread_rows(bc_all, bc_rows)
    for r in range(rows):
        bx[r] = jnp.broadcast_to(bc_rows[0:states, r : r + 1], (states, LANES))
        cx[r] = jnp.broadcast_to(bc_rows[states : 2 * states, r : r + 1], (states, LANES))
    ex_one[2].wait_recv()
    low = low_all[...].reshape(rows, rank)
    pre_value = dot_nn(low, dt_full[...]) + dt_bias[...]
    pre[...] = pre_value
    step_value = jnp.maximum(pre_value, 0.0) + jnp.log1p(jnp.exp(-jnp.abs(pre_value)))
    step[...] = step_value
    u_rows[...] = step_value * xconv[...].astype(F32)

    wide = 2 * LANES

    def across_lanes(tile, count):
        return jnp.concatenate([tile] * count, 1)

    for block in range(width // wide):
        lanes = slice(block * wide, (block + 1) * wide)
        rate = rate_all[:, lanes]

        def alone(k, carried):
            ahead = list(carried[:seqs])
            behind = list(carried[seqs:])
            for s in range(seqs):
                first = s * tokens + k * 8
                last = s * tokens + tokens - (k + 1) * 8
                step_f, u_f = views((step, u_rows), first, 8, lanes)
                step_b, gy_b = views((step, gy), last, 8, lanes)
                for i in range(8):
                    now = jnp.exp(step_f[i : i + 1, :] * rate)
                    b_tile = across_lanes(bx[first + i], 2)
                    ahead[s] = now * ahead[s] + b_tile * u_f[i : i + 1, :]
                    j = 7 - i
                    now = jnp.exp(step_b[j : j + 1, :] * rate)
                    c_tile = across_lanes(cx[last + j], 2)
                    behind[s] = now * (c_tile * gy_b[j : j + 1, :] + behind[s])
            return tuple(ahead + behind)

        zero = jnp.zeros((states, wide), F32)
        ends = lax.fori_loop(0, tokens // 8, alone, (zero,) * (2 * seqs))
        for s in range(seqs):
            total = jnp.sum(step[s * tokens : (s + 1) * tokens, lanes], axis=0, keepdims=True)
            passing = jnp.exp(rate * total)
            for n in range(states):
                parts[s * states + n, 0:1, lanes] = ends[s][n : n + 1, :]
                parts[s * states + n, 1:2, lanes] = ends[seqs + s][n : n + 1, :]
                parts[s * states + n, 2:3, lanes] = passing[n : n + 1, :]

    ex_parts.start()
    slots[me] = parts[me]
    span = CHUNK * states
    turns = tokens // CHUNK
    spread = (
        (lax.broadcasted_iota(jnp.int32, (states, span), 1) & (states - 1))
        == lax.broadcasted_iota(jnp.int32, (states, span), 0)
    ).astype(F32)
    spread_half = spread.astype(BF16)
    own = (
        lax.shift_right_logical(
            lax.broadcasted_iota(jnp.int32, (rows, span), 1), states.bit_length() - 1
        )
        == (lax.broadcasted_iota(jnp.int32, (rows, span), 0) & (CHUNK - 1))
    ).astype(F32)
    across = jnp.transpose(bc_rows[...])
    b_diag[...] = (dot_nn(across[:, :states].astype(BF16), spread_half) * own).astype(BF16)
    c_diag[...] = (dot_nn(across[:, states:].astype(BF16), spread_half) * own).astype(BF16)
    own = own[:CHUNK]
    fold = own.astype(BF16)
    lanes_row = lax.broadcasted_iota(jnp.int32, (LANES, 2 * span), 0)
    lanes_col = lax.broadcasted_iota(jnp.int32, (LANES, 2 * span), 1)
    target = (lanes_col & (states - 1)) + jnp.where(lanes_col < span, 0, states)
    gather_bc = (lanes_row == target).astype(F32).astype(BF16)
    u_half[...] = u_rows[...].astype(BF16)
    gy_half[...] = gy[...].astype(BF16)

    def prepare(k, carry):
        step_v, u_v = views((step, u_rows), k * 8, 8, slice(0, width))
        for i in range(8):
            r = k * 8 + i
            decays[r] = jnp.exp(step_v[i : i + 1, :] * rate_all)
            b_in[r] = across_lanes(bx[r], width // LANES) * u_v[i : i + 1, :]
        return carry

    lax.fori_loop(0, rows // 8, prepare, 0)
    ex_parts.wait_recv()

    def prefix(k, carried):
        ahead, behind = carried
        late = dp - 1 - k
        found[k, 0:1, :] = ahead
        found[late, 1:2, :] = behind
        ahead = slots[k, 2:3, :] * ahead + slots[k, 0:1, :]
        behind = slots[late, 2:3, :] * behind + slots[late, 1:2, :]
        return (ahead, behind)

    zero = jnp.zeros((1, width), F32)
    lax.fori_loop(0, dp, prefix, (zero, zero))
    ex_found.start()
    incoming[me] = found[me]

    def prepare_back(k, carry):
        gy_v = views((gy,), k * 8, 8, slice(0, width))[0]
        for i in range(8):
            r = k * 8 + i
            c_in[r] = across_lanes(cx[r], width // LANES) * gy_v[i : i + 1, :]
        return carry

    lax.fori_loop(0, rows // 8, prepare_back, 0)
    ex_found.wait_recv()
    for s in range(seqs):
        for n in range(states):
            begin[s, n : n + 1, :] = incoming[s * states + n, 0:1, :]
            begin[seqs + s, n : n + 1, :] = incoming[s * states + n, 1:2, :]
        hist[s, 0] = begin[s].astype(BF16)

    def forward(k, carried):
        carried = list(carried)
        for s in range(seqs):
            for i in range(8):
                t = k * 8 + i
                carried[s] = decays[s * tokens + t] * carried[s] + b_in[s * tokens + t]
                hist[s, t + 1] = carried[s].astype(BF16)
        return tuple(carried)

    lax.fori_loop(0, tokens // 8, forward, tuple(begin[s] for s in range(seqs)))

    def backward(k, carried):
        passed = list(carried[:seqs])
        rate_grad = carried[seqs]
        chunk = turns - 1 - k
        first = chunk * CHUNK
        folded = []
        rounded = []
        for s in range(seqs):
            here = pl.ds(pl.multiple_of(s * tokens + first, CHUNK), CHUNK)
            step_v = step.at[here, :]
            for i in reversed(range(CHUNK)):
                r = s * tokens + first + i
                adj = c_in[r] + passed[s]
                adjoint[s, i] = adj.astype(BF16)
                passed[s] = decays[r] * adj
                prev = passed[s] * hist[s, first + i].astype(F32) * rate_all
                prevs[s, i] = prev.astype(BF16)
                rate_grad = rate_grad + prev * step_v[i : i + 1, :]
            history = hist[s, pl.ds(first + 1, CHUNK)].reshape(span, width)
            adj = adjoint[s].reshape(span, width)
            b_adjoint = dot_nn(b_diag[here, :], adj)
            summed = dot_nn(fold, prevs[s].reshape(span, width))
            grad_b = dot_nt(u_half[here, :], adj) * own
            grad_c = dot_nt(gy_half[here, :], history) * own
            folded.append(jnp.concatenate([grad_b, grad_c], 1))
            x = xconv[here, :].astype(F32)
            grad_pre = (x * b_adjoint + summed) * lax.logistic(pre[here, :])
            g_rows[here, :] = grad_pre
            rounded.append(grad_pre.astype(BF16))
            g_half[here, :] = rounded[s]
            b_rows[here, :] = d_skip[...] * gy[here, :] + step[here, :] * b_adjoint
        folded = jnp.concatenate(folded, 0)
        coarse = folded.astype(BF16)
        fine = (folded - coarse.astype(F32)).astype(BF16)
        halves = dot_nt(jnp.concatenate([coarse, fine], 0), gather_bc)
        grad_bc = halves[: seqs * CHUNK] + halves[seqs * CHUNK :]
        low_grad = dot_nt(jnp.concatenate(rounded, 0), dt_full[...])
        message = jnp.concatenate([low_grad, grad_bc], 1).astype(BF16)
        for s in range(seqs):
            owner = s * turns + chunk
            part2[owner] = message[s * CHUNK : (s + 1) * CHUNK]

            @pl.when(mine != owner)
            def _():
                ex_two.start_one(owner)

            @pl.when(mine == owner)
            def _():
                slots2[mine] = part2[mine]

        return tuple(passed) + (rate_grad,)

    ends = lax.fori_loop(
        0,
        turns,
        backward,
        tuple(begin[seqs + s] for s in range(seqs)) + (jnp.zeros((states, width), F32),),
    )
    rate_sum = ends[seqs]

    dtw = dot_tn(low_all[...].reshape(rows, rank), g_half[...])
    for i in range(dp):
        dtw_part[i] = fold_lanes(dtw[i * part : (i + 1) * part]).astype(BF16)
    ex_dtw.start()
    dtw_slots[me] = dtw_part[me]
    x = xconv[...].astype(F32)
    sums = [rate_sum]
    sums.append(jnp.sum(g_rows[...], axis=0, keepdims=True))
    sums.append(jnp.sum(gy[...] * x, axis=0, keepdims=True))
    ex_two.wait_recv()

    def add_messages(k, total):
        return total + slots2[k].astype(F32)

    zero = jnp.zeros(slots2.shape[1:], F32)
    all2[mine] = lax.fori_loop(0, expert, add_messages, zero).astype(BF16)
    ex_three.start()
    for s in range(seqs):
        for k in range(turns):
            t = k * CHUNK
            here = slice(s * tokens + t, s * tokens + t + CHUNK)
            history = hist[s, t + 1 : t + 1 + CHUNK].reshape(span, width)
            y_rows[here, :] = dot_nn(c_diag[here, :], history)
    y_value = y_rows[...] + d_skip[...] * x
    gate_out[...] = (y_value * gate_factor[...]).astype(BF16).reshape(gate_out.shape)
    ex_three.wait_recv()

    grad_projected = all2[...].reshape(rows, all2.shape[2])
    x_flat = xconv[...]
    grad_conv = b_rows[...] + dot_nn(grad_projected, proj_full[...])
    state_terms = dot_tn(grad_projected[:, rank:], x_flat)
    value = preact[...]
    sig = lax.logistic(value)
    grad_pre = grad_conv * sig * (1.0 + value * (1.0 - sig))
    conv_terms = [jnp.zeros((1, width), F32) for k in range(taps)]
    for s in range(seqs):
        part_grad = grad_pre[s * tokens : (s + 1) * tokens]
        grads[s, 0:tokens, :] = part_grad
        edge_grad[8 * s : 8 * s + 8, :] = part_grad[0:8]
        for k in range(taps):
            first = 8 - reach + k
            conv_terms[k] = conv_terms[k] + jnp.sum(
                part_grad * padded[s, first : first + tokens, :], axis=0, keepdims=True
            )
    halo_back.start()
    pieces = [state_terms[i : i + 1] for i in range(2 * states)]
    pieces += conv_terms
    pieces.append(jnp.sum(grad_pre, axis=0, keepdims=True))
    pieces += [sums[0][i : i + 1] for i in range(states)]
    pieces += sums[1:]
    while len(pieces) < 2 * dp:
        pieces.append(jnp.zeros((1, width), F32))
    for i, piece in enumerate(pieces):
        small_part[i // 2, i % 2 : i % 2 + 1, :] = piece
    ex_small.start()
    small_slots[me] = small_part[me]
    pw = dot_tn(grad_projected[:, :rank], x_flat)
    for i in range(dp):
        pw_part[i] = fold_lanes(pw[i * part : (i + 1) * part]).astype(BF16)
    ex_pw.start()
    pw_slots[me] = pw_part[me]

    def add_slots(refs):
        def add(k, total):
            return tuple(t + ref[k].astype(F32) for t, ref in zip(total, refs))

        return lax.fori_loop(0, dp, add, tuple(jnp.zeros(ref.shape[1:], F32) for ref in refs))

    ex_dtw.wait_recv()
    dtw_out[...] = unfold_lanes(add_slots((dtw_slots,))[0])
    halo_back.wait_recv()
    keep = jnp.where(me == dp - 1, 0.0, 1.0).astype(F32)
    for s in range(seqs):
        grads[s, tokens:, :] = after[8 * s : 8 * s + 8, :] * keep
        result = jnp.zeros((tokens, width), F32)
        for k in range(taps):
            late = reach - k
            result = result + conv_weight[k : k + 1, :] * grads[s, late : late + tokens, :]
        gradx_out[s] = result.astype(BF16)
    ex_small.wait_recv()
    small_all[me] = add_slots((small_slots,))[0]
    ex_total.start()
    ex_pw.wait_recv()
    proj_out[...] = unfold_lanes(add_slots((pw_slots,))[0])
    for ex in (ex_proj, ex_extra, ex_dt) + ex_one + (ex_two, ex_three, ex_parts, ex_found, ex_dtw):
        ex.wait_send()
    halo.wait_send()
    halo_back.wait_send()
    ex_pw.wait_send()
    ex_small.wait_send()
    ex_total.wait_recv()
    ex_total.wait_send()


def output_body(
    states2, taps, gate, gradx, proj, dtw, small,
    gradx_out, gate_out, proj_out, state_out, dtw_out, weight_out, bias_out, dtb_out, alog_out, skip_out,
):
    gradx_out[...] = gradx[...]
    gate_out[...] = gate[...]
    proj_out[...] = proj[...]
    dtw_out[...] = dtw[...]
    states = states2 // 2
    targets = [(state_out, i) for i in range(states2)]
    targets += [(weight_out, i) for i in range(taps)]
    targets.append((bias_out, 0))
    targets += [(alog_out, i) for i in range(states)]
    targets += [(dtb_out, 0), (skip_out, 0)]
    for i, (target, row) in enumerate(targets):
        target[row : row + 1, :] = small[i // 2, i % 2 : i % 2 + 1, :]


def body(
    xin, zin, cotangent, conv_weight, conv_bias, proj_weight, dt_weight, dt_bias, a_log, d_skip
):
    dp = lax.axis_size("dp")
    expert = lax.axis_size("expert")
    seqs, tokens, width = xin.shape
    taps = conv_weight.shape[0]
    states = a_log.shape[0]
    rows = seqs * tokens
    part = dt_weight.shape[0]
    proj_rows = proj_weight.shape[0]
    rank = part * dp
    half = width // 2

    low_shape = (expert, rows // expert, rank)
    bc_shape = (expert, 2 * states // expert, rows)
    flat = (rows, width)
    cube = (seqs, tokens, width)
    fold = (2 * part, half)
    extra = (proj_rows - part, width)

    def f32(*shape):
        return pltpu.VMEM(shape, F32)

    def bf16(*shape):
        return pltpu.VMEM(shape, BF16)

    reduction = [bf16(*low_shape), f32(*bc_shape)] * 3
    scratch = [bf16(*fold), f32(*extra), bf16(*fold), bf16(8 * seqs, width)]
    scratch += [bf16(dp, *fold), f32(dp, *extra), bf16(dp, *fold), bf16(8 * seqs, width)]
    scratch += reduction + [bf16(expert, rows // expert, rank + LANES)] * 3
    scratch += [f32(dp, 3, width), f32(dp, 3, width), f32(dp, 2, width), f32(dp, 2, width)]
    scratch += [bf16(dp, *fold)] * 4 + [f32(dp, 2, width)] * 2 + [f32(8 * seqs, width)] * 2
    scratch += [f32(proj_rows * dp, width), bf16(rank + LANES, width), bf16(rank, width)]
    scratch += [f32(seqs, tokens + 8, width)] * 2
    scratch += [f32(*flat), bf16(*flat), f32(*flat), f32(*flat), f32(*flat), f32(*flat)]
    scratch += [f32(*flat)] * 4 + [bf16(*flat)] * 3 + [bf16(rows, CHUNK * states)] * 2
    scratch += [f32(rows, states, LANES)] * 2
    scratch += [f32(2 * states, rows), f32(2 * seqs, states, width)]
    scratch += [bf16(seqs, tokens + 1, states, width)] + [bf16(seqs, CHUNK, states, width)] * 2
    scratch += [f32(rows, states, width)] * 3
    scratch += [pltpu.SemaphoreType.DMA] * 34

    gate, gradx, proj, dtw, small = pl.pallas_call(
        functools.partial(core_body, dp, expert),
        out_shape=(
            sds(cube, BF16),
            sds(cube, BF16),
            sds((part, width), F32),
            sds((part, width), F32),
            sds((dp, 2, width), F32),
        ),
        in_specs=[whole] * 10,
        out_specs=(whole,) * 5,
        scratch_shapes=scratch,
        compiler_params=pltpu.CompilerParams(
            collective_id=1, has_side_effects=True, vmem_limit_bytes=VMEM_BYTES
        ),
        name="core",
    )(
        xin,
        zin,
        cotangent,
        conv_weight,
        conv_bias[None, :],
        proj_weight,
        dt_weight,
        dt_bias[None, :],
        a_log,
        d_skip[None, :],
    )
    row = sds((1, width), F32)
    results = pl.pallas_call(
        functools.partial(output_body, 2 * states, taps),
        out_shape=(
            sds(cube, BF16),
            sds(cube, BF16),
            sds((part, width), F32),
            sds((2 * states, width), F32),
            sds((part, width), F32),
            sds((taps, width), F32),
            row,
            row,
            sds((states, width), F32),
            row,
        ),
        in_specs=[whole] * 5,
        out_specs=(whole,) * 10,
        compiler_params=pltpu.CompilerParams(vmem_limit_bytes=VMEM_BYTES),
        name="outputs",
    )(gate, gradx, proj, dtw, small)
    results = list(results)
    for i in (6, 7, 9):
        results[i] = results[i].reshape(width)
    return tuple(results)


def solution(mesh):
    return jax.shard_map(
        body,
        mesh=mesh,
        in_specs=(
            P(None, "dp", "expert"),
            P(None, "dp", "expert"),
            P(None, "dp", "expert"),
            P(None, "expert"),
            P("expert"),
            P("dp", "expert"),
            P("dp", "expert"),
            P("expert"),
            P(None, "expert"),
            P("expert"),
        ),
        out_specs=(
            P(None, "dp", "expert"),
            P(None, "dp", "expert"),
            P("dp", "expert"),
            P(None, "expert"),
            P("dp", "expert"),
            P(None, "expert"),
            P("expert"),
            P("expert"),
            P(None, "expert"),
            P("expert"),
        ),
        check_vma=False,
    )
```

```python
import functools

import jax
import jax.numpy as jnp
from jax import lax
from jax.experimental import pallas as pl
from jax.experimental.pallas import tpu as pltpu
from jax.sharding import PartitionSpec as P

F32 = jnp.float32
BF16 = jnp.bfloat16
MESH = pl.DeviceIdType.MESH
LANES = 128
CHUNK = 16
VMEM_BYTES = 56 * 1024 * 1024

whole = pl.BlockSpec(memory_space=pltpu.VMEM)
sds = jax.ShapeDtypeStruct


def dot_nn(left, right, precision=None):
    return lax.dot_general(
        left, right, (((1,), (0,)), ((), ())), preferred_element_type=F32, precision=precision
    )


def dot_nt(left, right, precision=None):
    return lax.dot_general(
        left, right, (((1,), (1,)), ((), ())), preferred_element_type=F32, precision=precision
    )


def dot_tn(left, right):
    return lax.dot_general(left, right, (((0,), (0,)), ((), ())), preferred_element_type=F32)


TORUS = {"dp": (4, 8), "expert": (8, 2)}


def partners(axis, me):
    outer, inner = TORUS[axis]
    steps = [(a, b) for a in range(outer) for b in range(inner) if a + b > 0]
    steps.sort(key=lambda step: -min(step[0], outer - step[0]) - min(step[1], inner - step[1]))
    here, there = me // inner, lax.rem(me, inner)
    return [lax.rem(here + a, outer) * inner + lax.rem(there + b, inner) for a, b in steps]


def hail(axis, me):
    barrier = pltpu.get_barrier_semaphore()
    for peer in partners(axis, me):
        pl.semaphore_signal(barrier, inc=1, device_id={axis: peer}, device_id_type=MESH)


class Exchange:
    def __init__(self, axis, count, me, source, landing, sems):
        self.axis, self.count, self.me = axis, count, me
        self.source, self.landing = source, landing
        self.send_sem, self.recv_sem = sems

    def start_one(self, peer):
        pltpu.make_async_remote_copy(
            src_ref=self.source(peer),
            dst_ref=self.landing.at[self.me],
            send_sem=self.send_sem,
            recv_sem=self.recv_sem,
            device_id={self.axis: peer},
            device_id_type=MESH,
        ).start()

    def start(self):
        for peer in partners(self.axis, self.me):
            self.start_one(peer)

    def wait_bytes(self, sem):
        others = self.landing.at[pl.ds(0, self.count - 1)]
        pltpu.make_async_copy(others, others, sem).wait()

    def wait_recv(self):
        self.wait_bytes(self.recv_sem)

    def wait_send(self):
        self.wait_bytes(self.send_sem)


def fold_lanes(value):
    half = value.shape[1] // 2
    return jnp.concatenate([value[:, :half], value[:, half:]], 0)


def unfold_lanes(value):
    half = value.shape[0] // 2
    return jnp.concatenate([value[:half], value[half:]], 1)


def views(refs, first, count, lanes):
    first = pl.multiple_of(first, count)
    return [ref.at[pl.ds(first, count), lanes] for ref in refs]


def reduce_start(ex_low, ex_bc, low_slots, bc_slots, low, bc, me):
    ex_low.start()
    ex_bc.start()
    low_slots[me] = low[me]
    bc_slots[me] = bc[me]


def reduce_middle(ex, low_slots, bc_slots, low_all, bc_all, me, count):
    ex[0].wait_recv()
    ex[1].wait_recv()

    def add(k, total):
        return (total[0] + low_slots[k].astype(F32), total[1] + bc_slots[k])

    zero = (jnp.zeros(low_slots.shape[1:], F32), jnp.zeros(bc_slots.shape[1:], F32))
    low_sum, bc_sum = lax.fori_loop(0, count, add, zero)
    low_all[me] = low_sum.astype(BF16)
    bc_all[me] = bc_sum
    ex[2].start()
    ex[3].start()


def spread_rows(source, target):
    per = source.shape[1]
    for e in range(source.shape[0]):
        target[e * per : (e + 1) * per, :] = source[e]


def core_body(
    dp, expert,
    xin, zin, cot, conv_weight, conv_bias, proj_mine, dt_mine, dt_bias, a_log, d_skip,
    gate_out, gradx_out, proj_out, dtw_out, small_all,
    send_proj, send_extra, send_dt, send_edge, all_proj, all_extra, all_dt, front,
    low_part, bc_part, low_slots, bc_slots, low_all, bc_all,
    part2, slots2, all2,
    parts, slots, found, incoming,
    dtw_part, dtw_slots, pw_part, pw_slots, small_part, small_slots, edge_grad, after,
    proj_wide, proj_full, dt_full, padded, grads, preact, xconv, pre, step, gy, gate_factor,
    u_rows, y_rows, b_rows, g_rows, u_half, gy_half, g_half, b_diag, c_diag,
    bx, cx, bc_rows, begin, hist, adjoint, prevs, decays, b_in, c_in,
    *sems,
):
    seqs, tokens, width = zin.shape
    states = a_log.shape[0]
    taps = conv_weight.shape[0]
    reach = taps - 1
    rows = seqs * tokens
    rank = dt_full.shape[0]
    part = dt_mine.shape[0]
    proj_rows = proj_mine.shape[0]
    me = lax.axis_index("dp")
    mine = lax.axis_index("expert")
    hail("dp", me)
    hail("expert", mine)

    pairs = iter(range(0, len(sems), 2))

    def next_pair():
        i = next(pairs)
        return (sems[i], sems[i + 1])

    def over_dp(source, landing):
        return Exchange("dp", dp, me, source, landing, next_pair())

    def over_expert(source, landing):
        return Exchange("expert", expert, mine, source, landing, next_pair())

    def reduction(low, bc, low_in, bc_in, low_out, bc_out):
        return (
            over_expert(lambda p: low.at[p], low_in),
            over_expert(lambda p: bc.at[p], bc_in),
            over_expert(lambda p: low_out.at[mine], low_out),
            over_expert(lambda p: bc_out.at[mine], bc_out),
        )

    ex_proj = over_dp(lambda p: send_proj, all_proj)
    ex_extra = over_dp(lambda p: send_extra, all_extra)
    ex_dt = over_dp(lambda p: send_dt, all_dt)
    ex_one = reduction(low_part, bc_part, low_slots, bc_slots, low_all, bc_all)
    ex_two = over_expert(lambda p: part2.at[p], slots2)
    ex_three = over_expert(lambda p: all2.at[mine], all2)
    ex_parts = over_dp(lambda p: parts.at[p], slots)
    ex_found = over_dp(lambda p: found.at[p], incoming)
    ex_dtw = over_dp(lambda p: dtw_part.at[p], dtw_slots)
    ex_pw = over_dp(lambda p: pw_part.at[p], pw_slots)
    ex_small = over_dp(lambda p: small_part.at[p], small_slots)
    ex_total = over_dp(lambda p: small_all.at[me], small_all)

    def neighbour(source, target, distance):
        pair = next_pair()
        return pltpu.make_async_remote_copy(
            src_ref=source,
            dst_ref=target,
            send_sem=pair[0],
            recv_sem=pair[1],
            device_id={"dp": lax.rem(me + dp + distance, dp)},
            device_id_type=MESH,
        )

    halo = neighbour(send_edge, front, 1)
    halo_back = neighbour(edge_grad, after, -1)

    proj32 = proj_mine[...].astype(F32)
    send_proj[...] = fold_lanes(proj32[:part]).astype(BF16)
    send_extra[...] = proj32[part:]
    send_dt[...] = fold_lanes(dt_mine[...].astype(F32)).astype(BF16)
    send_edge[...] = jnp.concatenate(
        [xin[s, tokens - 16 :, :].astype(F32)[8:] for s in range(seqs)], 0
    ).astype(BF16)
    all_proj[me] = send_proj[...]
    all_extra[me] = send_extra[...]
    all_dt[me] = send_dt[...]
    for s in range(seqs):
        here = slice(s * tokens, (s + 1) * tokens)
        z = zin[s].astype(F32)
        g = cot[s].astype(F32)
        sig = lax.logistic(z)
        gy[here, :] = g * z * sig
        gate_factor[here, :] = g * sig * (1.0 + z * (1.0 - sig))
        padded[s, 8:, :] = xin[s].astype(F32)
    rate_all = -jnp.exp(a_log[...])
    pl.semaphore_wait(pltpu.get_barrier_semaphore(), dp + expert - 2)

    halo.start()
    ex_proj.start()
    ex_extra.start()
    ex_dt.start()

    halo.wait_recv()
    keep = jnp.where(me == 0, 0.0, 1.0).astype(F32)
    lead = front[...].astype(F32) * keep
    for s in range(seqs):
        padded[s, 8 - reach : 8, :] = lead[8 * s + 8 - reach : 8 * s + 8, :]
        value = conv_bias[...] + jnp.zeros((tokens, width), F32)
        for k in range(taps):
            first = 8 - reach + k
            value = value + conv_weight[k : k + 1, :] * padded[s, first : first + tokens, :]
        here = slice(s * tokens, (s + 1) * tokens)
        preact[here, :] = value
        xconv[here, :] = (value * lax.logistic(value)).astype(BF16)
    ex_proj.wait_recv()
    ex_extra.wait_recv()
    for i in range(dp):
        proj_wide[i * proj_rows : i * proj_rows + part, :] = unfold_lanes(all_proj[i].astype(F32))
        proj_wide[i * proj_rows + part : (i + 1) * proj_rows, :] = all_extra[i]
    total = rank + 2 * states
    proj_full[0:total, :] = proj_wide[...].astype(BF16)
    proj_full[total:, :] = jnp.zeros((proj_full.shape[0] - total, width), BF16)
    x_flat = xconv[...]
    bc = dot_nt(proj_full[rank:total, :], x_flat)
    per = bc_part.shape[1]
    for e in range(expert):
        bc_part[e] = bc[e * per : (e + 1) * per, :]
    low_part[...] = dot_nt(x_flat, proj_full[0:rank, :]).reshape(low_part.shape).astype(BF16)
    reduce_start(ex_one[0], ex_one[1], low_slots, bc_slots, low_part, bc_part, mine)
    ex_dt.wait_recv()
    for i in range(0, dp, 2):
        pair = [unfold_lanes(all_dt[i + j].astype(F32)) for j in range(2)]
        dt_full[i * part : (i + 2) * part, :] = jnp.concatenate(pair, 0).astype(BF16)
    reduce_middle(ex_one, low_slots, bc_slots, low_all, bc_all, mine, expert)
    ex_one[3].wait_recv()
    spread_rows(bc_all, bc_rows)
    for r in range(rows):
        bx[r] = jnp.broadcast_to(bc_rows[0:states, r : r + 1], (states, LANES))
        cx[r] = jnp.broadcast_to(bc_rows[states : 2 * states, r : r + 1], (states, LANES))
    ex_one[2].wait_recv()
    low = low_all[...].reshape(rows, rank)
    pre_value = dot_nn(low, dt_full[...]) + dt_bias[...]
    pre[...] = pre_value
    step_value = jnp.maximum(pre_value, 0.0) + jnp.log1p(jnp.exp(-jnp.abs(pre_value)))
    step[...] = step_value
    u_rows[...] = step_value * xconv[...].astype(F32)

    wide = 2 * LANES

    def across_lanes(tile, count):
        return jnp.concatenate([tile] * count, 1)

    for block in range(width // wide):
        lanes = slice(block * wide, (block + 1) * wide)
        rate = rate_all[:, lanes]

        def alone(k, carried):
            ahead = list(carried)
            for s in range(seqs):
                first = s * tokens + k * 8
                step_f, u_f = views((step, u_rows), first, 8, lanes)
                for i in range(8):
                    now = jnp.exp(step_f[i : i + 1, :] * rate)
                    decays[first + i, :, lanes] = now
                    b_tile = across_lanes(bx[first + i], 2)
                    ahead[s] = now * ahead[s] + b_tile * u_f[i : i + 1, :]
            return tuple(ahead)

        def alone_back(k, carried):
            behind = list(carried)
            for s in range(seqs):
                last = s * tokens + tokens - (k + 1) * 8
                gy_b = views((gy,), last, 8, lanes)[0]
                for j in reversed(range(8)):
                    now = decays[last + j, :, lanes]
                    c_tile = across_lanes(cx[last + j], 2)
                    behind[s] = now * (c_tile * gy_b[j : j + 1, :] + behind[s])
            return tuple(behind)

        zero = jnp.zeros((states, wide), F32)
        ends = lax.fori_loop(0, tokens // 8, alone, (zero,) * seqs)
        ends = ends + lax.fori_loop(0, tokens // 8, alone_back, (zero,) * seqs)
        for s in range(seqs):
            total = jnp.sum(step[s * tokens : (s + 1) * tokens, lanes], axis=0, keepdims=True)
            passing = jnp.exp(rate * total)
            for n in range(states):
                parts[s * states + n, 0:1, lanes] = ends[s][n : n + 1, :]
                parts[s * states + n, 1:2, lanes] = ends[seqs + s][n : n + 1, :]
                parts[s * states + n, 2:3, lanes] = passing[n : n + 1, :]

    ex_parts.start()
    slots[me] = parts[me]
    span = CHUNK * states
    turns = tokens // CHUNK
    spread = (
        (lax.broadcasted_iota(jnp.int32, (states, span), 1) & (states - 1))
        == lax.broadcasted_iota(jnp.int32, (states, span), 0)
    ).astype(F32)
    spread_half = spread.astype(BF16)
    own = (
        lax.shift_right_logical(
            lax.broadcasted_iota(jnp.int32, (rows, span), 1), states.bit_length() - 1
        )
        == (lax.broadcasted_iota(jnp.int32, (rows, span), 0) & (CHUNK - 1))
    ).astype(F32)
    across = jnp.transpose(bc_rows[...])
    b_diag[...] = (dot_nn(across[:, :states].astype(BF16), spread_half) * own).astype(BF16)
    c_diag[...] = (dot_nn(across[:, states:].astype(BF16), spread_half) * own).astype(BF16)
    own = own[:CHUNK]
    fold = own.astype(BF16)
    lanes_row = lax.broadcasted_iota(jnp.int32, (LANES, 2 * span), 0)
    lanes_col = lax.broadcasted_iota(jnp.int32, (LANES, 2 * span), 1)
    target = (lanes_col & (states - 1)) + jnp.where(lanes_col < span, 0, states)
    gather_bc = (lanes_row == target).astype(F32).astype(BF16)
    u_half[...] = u_rows[...].astype(BF16)
    gy_half[...] = gy[...].astype(BF16)

    def prepare(k, carry):
        u_v = views((u_rows,), k * 8, 8, slice(0, width))[0]
        for i in range(8):
            r = k * 8 + i
            b_in[r] = across_lanes(bx[r], width // LANES) * u_v[i : i + 1, :]
        return carry

    lax.fori_loop(0, rows // 8, prepare, 0)
    ex_parts.wait_recv()

    def prefix(k, carried):
        ahead, behind = carried
        late = dp - 1 - k
        found[k, 0:1, :] = ahead
        found[late, 1:2, :] = behind
        ahead = slots[k, 2:3, :] * ahead + slots[k, 0:1, :]
        behind = slots[late, 2:3, :] * behind + slots[late, 1:2, :]
        return (ahead, behind)

    zero = jnp.zeros((1, width), F32)
    lax.fori_loop(0, dp, prefix, (zero, zero))
    ex_found.start()
    incoming[me] = found[me]

    def prepare_back(k, carry):
        gy_v = views((gy,), k * 8, 8, slice(0, width))[0]
        for i in range(8):
            r = k * 8 + i
            c_in[r] = across_lanes(cx[r], width // LANES) * gy_v[i : i + 1, :]
        return carry

    lax.fori_loop(0, rows // 8, prepare_back, 0)
    ex_found.wait_recv()
    for s in range(seqs):
        for n in range(states):
            begin[s, n : n + 1, :] = incoming[s * states + n, 0:1, :]
            begin[seqs + s, n : n + 1, :] = incoming[s * states + n, 1:2, :]
        hist[s, 0] = begin[s].astype(BF16)

    def forward(k, carried):
        carried = list(carried)
        for s in range(seqs):
            for i in range(8):
                t = k * 8 + i
                carried[s] = decays[s * tokens + t] * carried[s] + b_in[s * tokens + t]
                hist[s, t + 1] = carried[s].astype(BF16)
        return tuple(carried)

    lax.fori_loop(0, tokens // 8, forward, tuple(begin[s] for s in range(seqs)))

    def backward(k, carried):
        passed = list(carried[:seqs])
        rate_grad = carried[seqs]
        chunk = turns - 1 - k
        first = chunk * CHUNK
        folded = []
        rounded = []
        for s in range(seqs):
            here = pl.ds(pl.multiple_of(s * tokens + first, CHUNK), CHUNK)
            step_v = step.at[here, :]
            for i in reversed(range(CHUNK)):
                r = s * tokens + first + i
                adj = c_in[r] + passed[s]
                adjoint[s, i] = adj.astype(BF16)
                passed[s] = decays[r] * adj
                prev = passed[s] * hist[s, first + i].astype(F32) * rate_all
                prevs[s, i] = prev.astype(BF16)
                rate_grad = rate_grad + prev * step_v[i : i + 1, :]
            history = hist[s, pl.ds(first + 1, CHUNK)].reshape(span, width)
            adj = adjoint[s].reshape(span, width)
            b_adjoint = dot_nn(b_diag[here, :], adj)
            summed = dot_nn(fold, prevs[s].reshape(span, width))
            grad_b = dot_nt(u_half[here, :], adj) * own
            grad_c = dot_nt(gy_half[here, :], history) * own
            folded.append(jnp.concatenate([grad_b, grad_c], 1))
            x = xconv[here, :].astype(F32)
            grad_pre = (x * b_adjoint + summed) * lax.logistic(pre[here, :])
            g_rows[here, :] = grad_pre
            rounded.append(grad_pre.astype(BF16))
            g_half[here, :] = rounded[s]
            b_rows[here, :] = d_skip[...] * gy[here, :] + step[here, :] * b_adjoint
        folded = jnp.concatenate(folded, 0)
        coarse = folded.astype(BF16)
        fine = (folded - coarse.astype(F32)).astype(BF16)
        halves = dot_nt(jnp.concatenate([coarse, fine], 0), gather_bc)
        grad_bc = halves[: seqs * CHUNK] + halves[seqs * CHUNK :]
        low_grad = dot_nt(jnp.concatenate(rounded, 0), dt_full[...])
        message = jnp.concatenate([low_grad, grad_bc], 1).astype(BF16)
        for s in range(seqs):
            owner = s * turns + chunk
            part2[owner] = message[s * CHUNK : (s + 1) * CHUNK]

            @pl.when(mine != owner)
            def _():
                ex_two.start_one(owner)

            @pl.when(mine == owner)
            def _():
                slots2[mine] = part2[mine]

        return tuple(passed) + (rate_grad,)

    ends = lax.fori_loop(
        0,
        turns,
        backward,
        tuple(begin[seqs + s] for s in range(seqs)) + (jnp.zeros((states, width), F32),),
    )
    rate_sum = ends[seqs]

    dtw = dot_tn(low_all[...].reshape(rows, rank), g_half[...])
    for i in range(dp):
        dtw_part[i] = fold_lanes(dtw[i * part : (i + 1) * part]).astype(BF16)
    ex_dtw.start()
    dtw_slots[me] = dtw_part[me]
    x = xconv[...].astype(F32)
    sums = [rate_sum]
    sums.append(jnp.sum(g_rows[...], axis=0, keepdims=True))
    sums.append(jnp.sum(gy[...] * x, axis=0, keepdims=True))
    ex_two.wait_recv()

    def add_messages(k, total):
        return total + slots2[k].astype(F32)

    zero = jnp.zeros(slots2.shape[1:], F32)
    all2[mine] = lax.fori_loop(0, expert, add_messages, zero).astype(BF16)
    ex_three.start()
    for s in range(seqs):
        for k in range(turns):
            t = k * CHUNK
            here = slice(s * tokens + t, s * tokens + t + CHUNK)
            history = hist[s, t + 1 : t + 1 + CHUNK].reshape(span, width)
            y_rows[here, :] = dot_nn(c_diag[here, :], history)
    y_value = y_rows[...] + d_skip[...] * x
    gate_out[...] = (y_value * gate_factor[...]).astype(BF16).reshape(gate_out.shape)
    ex_three.wait_recv()

    grad_projected = all2[...].reshape(rows, all2.shape[2])
    x_flat = xconv[...]
    grad_conv = b_rows[...] + dot_nn(grad_projected, proj_full[...])
    state_terms = dot_tn(grad_projected[:, rank:], x_flat)
    value = preact[...]
    sig = lax.logistic(value)
    grad_pre = grad_conv * sig * (1.0 + value * (1.0 - sig))
    conv_terms = [jnp.zeros((1, width), F32) for k in range(taps)]
    for s in range(seqs):
        part_grad = grad_pre[s * tokens : (s + 1) * tokens]
        grads[s, 0:tokens, :] = part_grad
        edge_grad[8 * s : 8 * s + 8, :] = part_grad[0:8]
        for k in range(taps):
            first = 8 - reach + k
            conv_terms[k] = conv_terms[k] + jnp.sum(
                part_grad * padded[s, first : first + tokens, :], axis=0, keepdims=True
            )
    halo_back.start()
    pieces = [state_terms[i : i + 1] for i in range(2 * states)]
    pieces += conv_terms
    pieces.append(jnp.sum(grad_pre, axis=0, keepdims=True))
    pieces += [sums[0][i : i + 1] for i in range(states)]
    pieces += sums[1:]
    while len(pieces) < 2 * dp:
        pieces.append(jnp.zeros((1, width), F32))
    for i, piece in enumerate(pieces):
        small_part[i // 2, i % 2 : i % 2 + 1, :] = piece
    ex_small.start()
    small_slots[me] = small_part[me]
    pw = dot_tn(grad_projected[:, :rank], x_flat)
    for i in range(dp):
        pw_part[i] = fold_lanes(pw[i * part : (i + 1) * part]).astype(BF16)
    ex_pw.start()
    pw_slots[me] = pw_part[me]

    def add_slots(refs):
        def add(k, total):
            return tuple(t + ref[k].astype(F32) for t, ref in zip(total, refs))

        return lax.fori_loop(0, dp, add, tuple(jnp.zeros(ref.shape[1:], F32) for ref in refs))

    ex_dtw.wait_recv()
    dtw_out[...] = unfold_lanes(add_slots((dtw_slots,))[0])
    halo_back.wait_recv()
    keep = jnp.where(me == dp - 1, 0.0, 1.0).astype(F32)
    for s in range(seqs):
        grads[s, tokens:, :] = after[8 * s : 8 * s + 8, :] * keep
        result = jnp.zeros((tokens, width), F32)
        for k in range(taps):
            late = reach - k
            result = result + conv_weight[k : k + 1, :] * grads[s, late : late + tokens, :]
        gradx_out[s] = result.astype(BF16)
    ex_small.wait_recv()
    small_all[me] = add_slots((small_slots,))[0]
    ex_total.start()
    ex_pw.wait_recv()
    proj_out[...] = unfold_lanes(add_slots((pw_slots,))[0])
    for ex in (ex_proj, ex_extra, ex_dt) + ex_one + (ex_two, ex_three, ex_parts, ex_found, ex_dtw):
        ex.wait_send()
    halo.wait_send()
    halo_back.wait_send()
    ex_pw.wait_send()
    ex_small.wait_send()
    ex_total.wait_recv()
    ex_total.wait_send()


def output_body(
    states2, taps, gate, gradx, proj, dtw, small,
    gradx_out, gate_out, proj_out, state_out, dtw_out, weight_out, bias_out, dtb_out, alog_out, skip_out,
):
    gradx_out[...] = gradx[...]
    gate_out[...] = gate[...]
    proj_out[...] = proj[...]
    dtw_out[...] = dtw[...]
    states = states2 // 2
    targets = [(state_out, i) for i in range(states2)]
    targets += [(weight_out, i) for i in range(taps)]
    targets.append((bias_out, 0))
    targets += [(alog_out, i) for i in range(states)]
    targets += [(dtb_out, 0), (skip_out, 0)]
    for i, (target, row) in enumerate(targets):
        target[row : row + 1, :] = small[i // 2, i % 2 : i % 2 + 1, :]


def body(
    xin, zin, cotangent, conv_weight, conv_bias, proj_weight, dt_weight, dt_bias, a_log, d_skip
):
    dp = lax.axis_size("dp")
    expert = lax.axis_size("expert")
    seqs, tokens, width = xin.shape
    taps = conv_weight.shape[0]
    states = a_log.shape[0]
    rows = seqs * tokens
    part = dt_weight.shape[0]
    proj_rows = proj_weight.shape[0]
    rank = part * dp
    half = width // 2

    low_shape = (expert, rows // expert, rank)
    bc_shape = (expert, 2 * states // expert, rows)
    flat = (rows, width)
    cube = (seqs, tokens, width)
    fold = (2 * part, half)
    extra = (proj_rows - part, width)

    def f32(*shape):
        return pltpu.VMEM(shape, F32)

    def bf16(*shape):
        return pltpu.VMEM(shape, BF16)

    reduction = [bf16(*low_shape), f32(*bc_shape)] * 3
    scratch = [bf16(*fold), f32(*extra), bf16(*fold), bf16(8 * seqs, width)]
    scratch += [bf16(dp, *fold), f32(dp, *extra), bf16(dp, *fold), bf16(8 * seqs, width)]
    scratch += reduction + [bf16(expert, rows // expert, rank + LANES)] * 3
    scratch += [f32(dp, 3, width), f32(dp, 3, width), f32(dp, 2, width), f32(dp, 2, width)]
    scratch += [bf16(dp, *fold)] * 4 + [f32(dp, 2, width)] * 2 + [f32(8 * seqs, width)] * 2
    scratch += [f32(proj_rows * dp, width), bf16(rank + LANES, width), bf16(rank, width)]
    scratch += [f32(seqs, tokens + 8, width)] * 2
    scratch += [f32(*flat), bf16(*flat), f32(*flat), f32(*flat), f32(*flat), f32(*flat)]
    scratch += [f32(*flat)] * 4 + [bf16(*flat)] * 3 + [bf16(rows, CHUNK * states)] * 2
    scratch += [f32(rows, states, LANES)] * 2
    scratch += [f32(2 * states, rows), f32(2 * seqs, states, width)]
    scratch += [bf16(seqs, tokens + 1, states, width)] + [bf16(seqs, CHUNK, states, width)] * 2
    scratch += [f32(rows, states, width)] * 3
    scratch += [pltpu.SemaphoreType.DMA] * 34

    gate, gradx, proj, dtw, small = pl.pallas_call(
        functools.partial(core_body, dp, expert),
        out_shape=(
            sds(cube, BF16),
            sds(cube, BF16),
            sds((part, width), F32),
            sds((part, width), F32),
            sds((dp, 2, width), F32),
        ),
        in_specs=[whole] * 10,
        out_specs=(whole,) * 5,
        scratch_shapes=scratch,
        compiler_params=pltpu.CompilerParams(
            collective_id=1, has_side_effects=True, vmem_limit_bytes=VMEM_BYTES
        ),
        name="core",
    )(
        xin,
        zin,
        cotangent,
        conv_weight,
        conv_bias[None, :],
        proj_weight,
        dt_weight,
        dt_bias[None, :],
        a_log,
        d_skip[None, :],
    )
    row = sds((1, width), F32)
    results = pl.pallas_call(
        functools.partial(output_body, 2 * states, taps),
        out_shape=(
            sds(cube, BF16),
            sds(cube, BF16),
            sds((part, width), F32),
            sds((2 * states, width), F32),
            sds((part, width), F32),
            sds((taps, width), F32),
            row,
            row,
            sds((states, width), F32),
            row,
        ),
        in_specs=[whole] * 5,
        out_specs=(whole,) * 10,
        compiler_params=pltpu.CompilerParams(vmem_limit_bytes=VMEM_BYTES),
        name="outputs",
    )(gate, gradx, proj, dtw, small)
    results = list(results)
    for i in (6, 7, 9):
        results[i] = results[i].reshape(width)
    return tuple(results)


def solution(mesh):
    return jax.shard_map(
        body,
        mesh=mesh,
        in_specs=(
            P(None, "dp", "expert"),
            P(None, "dp", "expert"),
            P(None, "dp", "expert"),
            P(None, "expert"),
            P("expert"),
            P("dp", "expert"),
            P("dp", "expert"),
            P("expert"),
            P(None, "expert"),
            P("expert"),
        ),
        out_specs=(
            P(None, "dp", "expert"),
            P(None, "dp", "expert"),
            P("dp", "expert"),
            P(None, "expert"),
            P("dp", "expert"),
            P(None, "expert"),
            P("expert"),
            P("expert"),
            P(None, "expert"),
            P("expert"),
        ),
        check_vma=False,
    )
```

```python
import functools

import jax
import jax.numpy as jnp
from jax import lax
from jax.experimental import pallas as pl
from jax.experimental.pallas import tpu as pltpu
from jax.sharding import PartitionSpec as P

F32 = jnp.float32
BF16 = jnp.bfloat16
MESH = pl.DeviceIdType.MESH
LANES = 128
CHUNK = 16
VMEM_BYTES = 56 * 1024 * 1024

whole = pl.BlockSpec(memory_space=pltpu.VMEM)
sds = jax.ShapeDtypeStruct


def dot_nn(left, right, precision=None):
    return lax.dot_general(
        left, right, (((1,), (0,)), ((), ())), preferred_element_type=F32, precision=precision
    )


def dot_nt(left, right, precision=None):
    return lax.dot_general(
        left, right, (((1,), (1,)), ((), ())), preferred_element_type=F32, precision=precision
    )


def dot_tn(left, right):
    return lax.dot_general(left, right, (((0,), (0,)), ((), ())), preferred_element_type=F32)


TORUS = {"dp": (4, 8), "expert": (8, 2)}


def partners(axis, me):
    outer, inner = TORUS[axis]
    steps = [(a, b) for a in range(outer) for b in range(inner) if a + b > 0]
    steps.sort(key=lambda step: -min(step[0], outer - step[0]) - min(step[1], inner - step[1]))
    here, there = me // inner, lax.rem(me, inner)
    return [lax.rem(here + a, outer) * inner + lax.rem(there + b, inner) for a, b in steps]


def hail(axis, me):
    barrier = pltpu.get_barrier_semaphore()
    for peer in partners(axis, me):
        pl.semaphore_signal(barrier, inc=1, device_id={axis: peer}, device_id_type=MESH)


class Exchange:
    def __init__(self, axis, count, me, source, landing, sems):
        self.axis, self.count, self.me = axis, count, me
        self.source, self.landing = source, landing
        self.send_sem, self.recv_sem = sems

    def start_one(self, peer):
        pltpu.make_async_remote_copy(
            src_ref=self.source(peer),
            dst_ref=self.landing.at[self.me],
            send_sem=self.send_sem,
            recv_sem=self.recv_sem,
            device_id={self.axis: peer},
            device_id_type=MESH,
        ).start()

    def start(self):
        for peer in partners(self.axis, self.me):
            self.start_one(peer)

    def wait_bytes(self, sem):
        others = self.landing.at[pl.ds(0, self.count - 1)]
        pltpu.make_async_copy(others, others, sem).wait()

    def wait_recv(self):
        self.wait_bytes(self.recv_sem)

    def wait_send(self):
        self.wait_bytes(self.send_sem)


def fold_lanes(value):
    half = value.shape[1] // 2
    return jnp.concatenate([value[:, :half], value[:, half:]], 0)


def unfold_lanes(value):
    half = value.shape[0] // 2
    return jnp.concatenate([value[:half], value[half:]], 1)


def views(refs, first, count, lanes):
    first = pl.multiple_of(first, count)
    return [ref.at[pl.ds(first, count), lanes] for ref in refs]


def reduce_start(ex_low, low_slots, bc_slots, low, bc, me):
    ex_low.start()
    low_slots[me] = low[me]
    bc_slots[me] = bc[me]


def reduce_middle(ex, low_slots, bc_slots, low_all, bc_all, me, count):
    ex[0].wait_recv()
    ex[1].wait_recv()

    def add(k, total):
        return (total[0] + low_slots[k].astype(F32), total[1] + bc_slots[k])

    zero = (jnp.zeros(low_slots.shape[1:], F32), jnp.zeros(bc_slots.shape[1:], F32))
    low_sum, bc_sum = lax.fori_loop(0, count, add, zero, unroll=8)
    low_all[me] = low_sum.astype(BF16)
    bc_all[me] = bc_sum
    ex[3].start()
    ex[2].start()


def spread_rows(source, target):
    per = source.shape[1]
    for e in range(source.shape[0]):
        target[e * per : (e + 1) * per, :] = source[e]


def core_body(
    dp, expert,
    xin, zin, cot, conv_weight, conv_bias, proj_mine, dt_mine, dt_bias, a_log, d_skip,
    gate_out, gradx_out, proj_out, dtw_out, small_all,
    send_proj, send_extra, send_dt, send_edge, all_proj, all_extra, all_dt, front,
    low_part, bc_part, low_slots, bc_slots, low_all, bc_all,
    part2, slots2, all2,
    parts, slots, found, incoming,
    dtw_part, dtw_slots, pw_part, pw_slots, small_part, small_slots, edge_grad, after,
    proj_wide, proj_full, dt_full, padded, grads, preact, xconv, pre, step, gy, gate_factor,
    u_rows, y_rows, b_rows, g_rows, u_half, gy_half, g_half, b_diag, c_diag,
    bx, cx, bc_rows, begin, hist, adjoint, prevs, decays, b_in, c_in,
    *sems,
):
    seqs, tokens, width = zin.shape
    states = a_log.shape[0]
    taps = conv_weight.shape[0]
    reach = taps - 1
    rows = seqs * tokens
    rank = dt_full.shape[0]
    part = dt_mine.shape[0]
    proj_rows = proj_mine.shape[0]
    me = lax.axis_index("dp")
    mine = lax.axis_index("expert")
    hail("dp", me)
    hail("expert", mine)

    pairs = iter(range(0, len(sems), 2))

    def next_pair():
        i = next(pairs)
        return (sems[i], sems[i + 1])

    def over_dp(source, landing):
        return Exchange("dp", dp, me, source, landing, next_pair())

    def over_expert(source, landing):
        return Exchange("expert", expert, mine, source, landing, next_pair())

    def reduction(low, bc, low_in, bc_in, low_out, bc_out):
        return (
            over_expert(lambda p: low.at[p], low_in),
            over_expert(lambda p: bc.at[p], bc_in),
            over_expert(lambda p: low_out.at[mine], low_out),
            over_expert(lambda p: bc_out.at[mine], bc_out),
        )

    ex_proj = over_dp(lambda p: send_proj, all_proj)
    ex_extra = over_dp(lambda p: send_extra, all_extra)
    ex_dt = over_dp(lambda p: send_dt, all_dt)
    ex_one = reduction(low_part, bc_part, low_slots, bc_slots, low_all, bc_all)
    ex_two = over_expert(lambda p: part2.at[p], slots2)
    ex_three = over_expert(lambda p: all2.at[mine], all2)
    ex_parts = over_dp(lambda p: parts.at[p], slots)
    ex_found = over_dp(lambda p: found.at[p], incoming)
    ex_dtw = over_dp(lambda p: dtw_part.at[p], dtw_slots)
    ex_pw = over_dp(lambda p: pw_part.at[p], pw_slots)
    ex_small = over_dp(lambda p: small_part.at[p], small_slots)
    ex_total = over_dp(lambda p: small_all.at[me], small_all)

    def neighbour(source, target, distance):
        pair = next_pair()
        return pltpu.make_async_remote_copy(
            src_ref=source,
            dst_ref=target,
            send_sem=pair[0],
            recv_sem=pair[1],
            device_id={"dp": lax.rem(me + dp + distance, dp)},
            device_id_type=MESH,
        )

    halo = neighbour(send_edge, front, 1)
    halo_back = neighbour(edge_grad, after, -1)

    proj32 = proj_mine[...].astype(F32)
    send_proj[...] = fold_lanes(proj32[:part]).astype(BF16)
    send_extra[...] = proj32[part:]
    send_dt[...] = fold_lanes(dt_mine[...].astype(F32)).astype(BF16)
    send_edge[...] = jnp.concatenate(
        [xin[s, tokens - 16 :, :].astype(F32)[8:] for s in range(seqs)], 0
    ).astype(BF16)
    all_proj[me] = send_proj[...]
    all_extra[me] = send_extra[...]
    all_dt[me] = send_dt[...]
    for s in range(seqs):
        here = slice(s * tokens, (s + 1) * tokens)
        z = zin[s].astype(F32)
        g = cot[s].astype(F32)
        sig = lax.logistic(z)
        gy[here, :] = g * z * sig
        gate_factor[here, :] = g * sig * (1.0 + z * (1.0 - sig))
        padded[s, 8:, :] = xin[s].astype(F32)
    rate_all = -jnp.exp(a_log[...])
    pl.semaphore_wait(pltpu.get_barrier_semaphore(), dp + expert - 2)

    halo.start()
    ex_extra.start()
    ex_proj.start()

    halo.wait_recv()
    keep = jnp.where(me == 0, 0.0, 1.0).astype(F32)
    lead = front[...].astype(F32) * keep
    for s in range(seqs):
        padded[s, 8 - reach : 8, :] = lead[8 * s + 8 - reach : 8 * s + 8, :]
        value = conv_bias[...] + jnp.zeros((tokens, width), F32)
        for k in range(taps):
            first = 8 - reach + k
            value = value + conv_weight[k : k + 1, :] * padded[s, first : first + tokens, :]
        here = slice(s * tokens, (s + 1) * tokens)
        preact[here, :] = value
        xconv[here, :] = (value * lax.logistic(value)).astype(BF16)
    ex_proj.wait_recv()
    ex_extra.wait_recv()
    for i in range(dp):
        proj_wide[i * proj_rows : i * proj_rows + part, :] = unfold_lanes(all_proj[i].astype(F32))
        proj_wide[i * proj_rows + part : (i + 1) * proj_rows, :] = all_extra[i]
    total = rank + 2 * states
    proj_full[0:total, :] = proj_wide[...].astype(BF16)
    proj_full[total:, :] = jnp.zeros((proj_full.shape[0] - total, width), BF16)
    x_flat = xconv[...]
    bc = dot_nt(proj_full[rank:total, :], x_flat)
    per = bc_part.shape[1]
    for e in range(expert):
        bc_part[e] = bc[e * per : (e + 1) * per, :]
    ex_one[1].start()
    low_part[...] = dot_nt(x_flat, proj_full[0:rank, :]).reshape(low_part.shape).astype(BF16)
    reduce_start(ex_one[0], low_slots, bc_slots, low_part, bc_part, mine)
    ex_dt.start()
    reduce_middle(ex_one, low_slots, bc_slots, low_all, bc_all, mine, expert)
    ex_dt.wait_recv()
    for i in range(0, dp, 2):
        pair = [unfold_lanes(all_dt[i + j].astype(F32)) for j in range(2)]
        dt_full[i * part : (i + 2) * part, :] = jnp.concatenate(pair, 0).astype(BF16)
    ex_one[3].wait_recv()
    ex_one[2].wait_recv()
    spread_rows(bc_all, bc_rows)
    for r in range(rows):
        bx[r] = jnp.broadcast_to(bc_rows[0:states, r : r + 1], (states, LANES))
        cx[r] = jnp.broadcast_to(bc_rows[states : 2 * states, r : r + 1], (states, LANES))
    low = low_all[...].reshape(rows, rank)
    pre_value = dot_nn(low, dt_full[...]) + dt_bias[...]
    pre[...] = pre_value
    step_value = jnp.maximum(pre_value, 0.0) + jnp.log1p(jnp.exp(-jnp.abs(pre_value)))
    step[...] = step_value
    u_rows[...] = step_value * xconv[...].astype(F32)

    wide = width

    def across_lanes(tile, count):
        return jnp.concatenate([tile] * count, 1)

    for block in range(width // wide):
        lanes = slice(block * wide, (block + 1) * wide)
        rate = rate_all[:, lanes]

        def alone(k, carried):
            ahead = list(carried)
            for s in range(seqs):
                first = s * tokens + k * 8
                step_f, u_f = views((step, u_rows), first, 8, lanes)
                for i in range(8):
                    now = jnp.exp(step_f[i : i + 1, :] * rate)
                    decays[first + i, :, lanes] = now
                    b_tile = across_lanes(bx[first + i], wide // LANES)
                    ahead[s] = now * ahead[s] + b_tile * u_f[i : i + 1, :]
            return tuple(ahead)

        def alone_back(k, carried):
            behind = list(carried)
            for s in range(seqs):
                last = s * tokens + tokens - (k + 1) * 8
                gy_b = views((gy,), last, 8, lanes)[0]
                for j in reversed(range(8)):
                    now = decays[last + j, :, lanes]
                    c_tile = across_lanes(cx[last + j], wide // LANES)
                    behind[s] = now * (c_tile * gy_b[j : j + 1, :] + behind[s])
            return tuple(behind)

        zero = jnp.zeros((states, wide), F32)
        ends = lax.fori_loop(0, tokens // 8, alone, (zero,) * seqs)
        ends = ends + lax.fori_loop(0, tokens // 8, alone_back, (zero,) * seqs)
        for s in range(seqs):
            total = jnp.sum(step[s * tokens : (s + 1) * tokens, lanes], axis=0, keepdims=True)
            passing = jnp.exp(rate * total)
            for n in range(states):
                parts[s * states + n, 0:1, lanes] = ends[s][n : n + 1, :]
                parts[s * states + n, 1:2, lanes] = ends[seqs + s][n : n + 1, :]
                parts[s * states + n, 2:3, lanes] = passing[n : n + 1, :]

    ex_parts.start()
    slots[me] = parts[me]
    span = CHUNK * states
    turns = tokens // CHUNK
    spread = (
        (lax.broadcasted_iota(jnp.int32, (states, span), 1) & (states - 1))
        == lax.broadcasted_iota(jnp.int32, (states, span), 0)
    ).astype(F32)
    spread_half = spread.astype(BF16)
    own = (
        lax.shift_right_logical(
            lax.broadcasted_iota(jnp.int32, (rows, span), 1), states.bit_length() - 1
        )
        == (lax.broadcasted_iota(jnp.int32, (rows, span), 0) & (CHUNK - 1))
    ).astype(F32)
    across = jnp.transpose(bc_rows[...])
    b_diag[...] = (dot_nn(across[:, :states].astype(BF16), spread_half) * own).astype(BF16)
    c_diag[...] = (dot_nn(across[:, states:].astype(BF16), spread_half) * own).astype(BF16)
    own = own[:CHUNK]
    fold = own.astype(BF16)
    lanes_row = lax.broadcasted_iota(jnp.int32, (LANES, 2 * span), 0)
    lanes_col = lax.broadcasted_iota(jnp.int32, (LANES, 2 * span), 1)
    target = (lanes_col & (states - 1)) + jnp.where(lanes_col < span, 0, states)
    gather_bc = (lanes_row == target).astype(F32).astype(BF16)
    u_half[...] = u_rows[...].astype(BF16)
    gy_half[...] = gy[...].astype(BF16)

    def prepare(k, carry):
        u_v = views((u_rows,), k * 8, 8, slice(0, width))[0]
        for i in range(8):
            r = k * 8 + i
            b_in[r] = across_lanes(bx[r], width // LANES) * u_v[i : i + 1, :]
        return carry

    lax.fori_loop(0, rows // 8, prepare, 0)
    ex_parts.wait_recv()

    def prefix(k, carried):
        ahead, behind = carried
        late = dp - 1 - k
        found[k, 0:1, :] = ahead
        found[late, 1:2, :] = behind
        ahead = slots[k, 2:3, :] * ahead + slots[k, 0:1, :]
        behind = slots[late, 2:3, :] * behind + slots[late, 1:2, :]
        return (ahead, behind)

    zero = jnp.zeros((1, width), F32)
    lax.fori_loop(0, dp, prefix, (zero, zero), unroll=8)
    ex_found.start()
    incoming[me] = found[me]

    def prepare_back(k, carry):
        gy_v = views((gy,), k * 8, 8, slice(0, width))[0]
        for i in range(8):
            r = k * 8 + i
            c_in[r] = across_lanes(cx[r], width // LANES) * gy_v[i : i + 1, :]
        return carry

    lax.fori_loop(0, rows // 8, prepare_back, 0)
    ex_found.wait_recv()
    for s in range(seqs):
        for n in range(states):
            begin[s, n : n + 1, :] = incoming[s * states + n, 0:1, :]
            begin[seqs + s, n : n + 1, :] = incoming[s * states + n, 1:2, :]
        hist[s, 0] = begin[s].astype(BF16)

    def forward(k, carried):
        carried = list(carried)
        for s in range(seqs):
            for i in range(8):
                t = k * 8 + i
                carried[s] = decays[s * tokens + t] * carried[s] + b_in[s * tokens + t]
                hist[s, t + 1] = carried[s].astype(BF16)
        return tuple(carried)

    lax.fori_loop(0, tokens // 8, forward, tuple(begin[s] for s in range(seqs)))

    def backward(k, carried):
        passed = list(carried[:seqs])
        rate_grad = carried[seqs]
        chunk = turns - 1 - k
        first = chunk * CHUNK
        folded = []
        rounded = []
        for s in range(seqs):
            here = pl.ds(pl.multiple_of(s * tokens + first, CHUNK), CHUNK)
            step_v = step.at[here, :]
            for i in reversed(range(CHUNK)):
                r = s * tokens + first + i
                adj = c_in[r] + passed[s]
                adjoint[s, i] = adj.astype(BF16)
                passed[s] = decays[r] * adj
                prev = passed[s] * hist[s, first + i].astype(F32) * rate_all
                prevs[s, i] = prev.astype(BF16)
                rate_grad = rate_grad + prev * step_v[i : i + 1, :]
            history = hist[s, pl.ds(first + 1, CHUNK)].reshape(span, width)
            adj = adjoint[s].reshape(span, width)
            b_adjoint = dot_nn(b_diag[here, :], adj)
            summed = dot_nn(fold, prevs[s].reshape(span, width))
            grad_b = dot_nt(u_half[here, :], adj) * own
            grad_c = dot_nt(gy_half[here, :], history) * own
            folded.append(jnp.concatenate([grad_b, grad_c], 1))
            x = xconv[here, :].astype(F32)
            grad_pre = (x * b_adjoint + summed) * lax.logistic(pre[here, :])
            g_rows[here, :] = grad_pre
            rounded.append(grad_pre.astype(BF16))
            g_half[here, :] = rounded[s]
            b_rows[here, :] = d_skip[...] * gy[here, :] + step[here, :] * b_adjoint
        folded = jnp.concatenate(folded, 0)
        coarse = folded.astype(BF16)
        fine = (folded - coarse.astype(F32)).astype(BF16)
        halves = dot_nt(jnp.concatenate([coarse, fine], 0), gather_bc)
        grad_bc = halves[: seqs * CHUNK] + halves[seqs * CHUNK :]
        low_grad = dot_nt(jnp.concatenate(rounded, 0), dt_full[...])
        message = jnp.concatenate([low_grad, grad_bc], 1).astype(BF16)
        for s in range(seqs):
            owner = s * turns + chunk
            part2[owner] = message[s * CHUNK : (s + 1) * CHUNK]

            @pl.when(mine != owner)
            def _():
                ex_two.start_one(owner)

            @pl.when(mine == owner)
            def _():
                slots2[mine] = part2[mine]

        return tuple(passed) + (rate_grad,)

    ends = lax.fori_loop(
        0,
        turns,
        backward,
        tuple(begin[seqs + s] for s in range(seqs)) + (jnp.zeros((states, width), F32),),
    )
    rate_sum = ends[seqs]

    dtw = dot_tn(low_all[...].reshape(rows, rank), g_half[...])
    for i in range(dp):
        dtw_part[i] = fold_lanes(dtw[i * part : (i + 1) * part]).astype(BF16)
    ex_dtw.start()
    dtw_slots[me] = dtw_part[me]
    x = xconv[...].astype(F32)
    sums = [rate_sum]
    sums.append(jnp.sum(g_rows[...], axis=0, keepdims=True))
    sums.append(jnp.sum(gy[...] * x, axis=0, keepdims=True))
    ex_two.wait_recv()

    def add_messages(k, total):
        return total + slots2[k].astype(F32)

    zero = jnp.zeros(slots2.shape[1:], F32)
    all2[mine] = lax.fori_loop(0, expert, add_messages, zero, unroll=8).astype(BF16)
    ex_three.start()
    for s in range(seqs):
        for k in range(turns):
            t = k * CHUNK
            here = slice(s * tokens + t, s * tokens + t + CHUNK)
            history = hist[s, t + 1 : t + 1 + CHUNK].reshape(span, width)
            y_rows[here, :] = dot_nn(c_diag[here, :], history)
    y_value = y_rows[...] + d_skip[...] * x
    gate_out[...] = (y_value * gate_factor[...]).astype(BF16).reshape(gate_out.shape)
    ex_three.wait_recv()

    grad_projected = all2[...].reshape(rows, all2.shape[2])
    x_flat = xconv[...]
    grad_conv = b_rows[...] + dot_nn(grad_projected, proj_full[...])
    state_terms = dot_tn(grad_projected[:, rank:], x_flat)
    value = preact[...]
    sig = lax.logistic(value)
    grad_pre = grad_conv * sig * (1.0 + value * (1.0 - sig))
    conv_terms = [jnp.zeros((1, width), F32) for k in range(taps)]
    for s in range(seqs):
        part_grad = grad_pre[s * tokens : (s + 1) * tokens]
        grads[s, 0:tokens, :] = part_grad
        edge_grad[8 * s : 8 * s + 8, :] = part_grad[0:8]
    halo_back.start()
    for s in range(seqs):
        part_grad = grad_pre[s * tokens : (s + 1) * tokens]
        for k in range(taps):
            first = 8 - reach + k
            conv_terms[k] = conv_terms[k] + jnp.sum(
                part_grad * padded[s, first : first + tokens, :], axis=0, keepdims=True
            )
    pieces = [state_terms[i : i + 1] for i in range(2 * states)]
    pieces += conv_terms
    pieces.append(jnp.sum(grad_pre, axis=0, keepdims=True))
    pieces += [sums[0][i : i + 1] for i in range(states)]
    pieces += sums[1:]
    while len(pieces) < 2 * dp:
        pieces.append(jnp.zeros((1, width), F32))
    for i, piece in enumerate(pieces):
        small_part[i // 2, i % 2 : i % 2 + 1, :] = piece
    ex_small.start()
    small_slots[me] = small_part[me]
    pw = dot_tn(grad_projected[:, :rank], x_flat)
    for i in range(dp):
        pw_part[i] = fold_lanes(pw[i * part : (i + 1) * part]).astype(BF16)
    ex_pw.start()
    pw_slots[me] = pw_part[me]

    def add_slots(refs):
        def add(k, total):
            return tuple(t + ref[k].astype(F32) for t, ref in zip(total, refs))

        zeros = tuple(jnp.zeros(ref.shape[1:], F32) for ref in refs)
        return lax.fori_loop(0, dp, add, zeros, unroll=8)

    ex_dtw.wait_recv()
    dtw_out[...] = unfold_lanes(add_slots((dtw_slots,))[0])
    halo_back.wait_recv()
    keep = jnp.where(me == dp - 1, 0.0, 1.0).astype(F32)
    for s in range(seqs):
        grads[s, tokens:, :] = after[8 * s : 8 * s + 8, :] * keep
        result = jnp.zeros((tokens, width), F32)
        for k in range(taps):
            late = reach - k
            result = result + conv_weight[k : k + 1, :] * grads[s, late : late + tokens, :]
        gradx_out[s] = result.astype(BF16)
    ex_small.wait_recv()
    small_all[me] = add_slots((small_slots,))[0]
    ex_total.start()
    ex_pw.wait_recv()
    proj_out[...] = unfold_lanes(add_slots((pw_slots,))[0])
    for ex in (ex_proj, ex_extra, ex_dt) + ex_one + (ex_two, ex_three, ex_parts, ex_found, ex_dtw):
        ex.wait_send()
    halo.wait_send()
    halo_back.wait_send()
    ex_pw.wait_send()
    ex_small.wait_send()
    ex_total.wait_recv()
    ex_total.wait_send()


def output_body(
    states2, taps, gate, gradx, proj, dtw, small,
    gradx_out, gate_out, proj_out, state_out, dtw_out, weight_out, bias_out, dtb_out, alog_out, skip_out,
):
    gradx_out[...] = gradx[...]
    gate_out[...] = gate[...]
    proj_out[...] = proj[...]
    dtw_out[...] = dtw[...]
    states = states2 // 2
    targets = [(state_out, i) for i in range(states2)]
    targets += [(weight_out, i) for i in range(taps)]
    targets.append((bias_out, 0))
    targets += [(alog_out, i) for i in range(states)]
    targets += [(dtb_out, 0), (skip_out, 0)]
    for i, (target, row) in enumerate(targets):
        target[row : row + 1, :] = small[i // 2, i % 2 : i % 2 + 1, :]


def body(
    xin, zin, cotangent, conv_weight, conv_bias, proj_weight, dt_weight, dt_bias, a_log, d_skip
):
    dp = lax.axis_size("dp")
    expert = lax.axis_size("expert")
    seqs, tokens, width = xin.shape
    taps = conv_weight.shape[0]
    states = a_log.shape[0]
    rows = seqs * tokens
    part = dt_weight.shape[0]
    proj_rows = proj_weight.shape[0]
    rank = part * dp
    half = width // 2

    low_shape = (expert, rows // expert, rank)
    bc_shape = (expert, 2 * states // expert, rows)
    flat = (rows, width)
    cube = (seqs, tokens, width)
    fold = (2 * part, half)
    extra = (proj_rows - part, width)

    def f32(*shape):
        return pltpu.VMEM(shape, F32)

    def bf16(*shape):
        return pltpu.VMEM(shape, BF16)

    reduction = [bf16(*low_shape), f32(*bc_shape)] * 3
    scratch = [bf16(*fold), f32(*extra), bf16(*fold), bf16(8 * seqs, width)]
    scratch += [bf16(dp, *fold), f32(dp, *extra), bf16(dp, *fold), bf16(8 * seqs, width)]
    scratch += reduction + [bf16(expert, rows // expert, rank + LANES)] * 3
    scratch += [f32(dp, 3, width), f32(dp, 3, width), f32(dp, 2, width), f32(dp, 2, width)]
    scratch += [bf16(dp, *fold)] * 4 + [f32(dp, 2, width)] * 2 + [f32(8 * seqs, width)] * 2
    scratch += [f32(proj_rows * dp, width), bf16(rank + LANES, width), bf16(rank, width)]
    scratch += [f32(seqs, tokens + 8, width)] * 2
    scratch += [f32(*flat), bf16(*flat), f32(*flat), f32(*flat), f32(*flat), f32(*flat)]
    scratch += [f32(*flat)] * 4 + [bf16(*flat)] * 3 + [bf16(rows, CHUNK * states)] * 2
    scratch += [f32(rows, states, LANES)] * 2
    scratch += [f32(2 * states, rows), f32(2 * seqs, states, width)]
    scratch += [bf16(seqs, tokens + 1, states, width)] + [bf16(seqs, CHUNK, states, width)] * 2
    scratch += [f32(rows, states, width)] * 3
    scratch += [pltpu.SemaphoreType.DMA] * 34

    gate, gradx, proj, dtw, small = pl.pallas_call(
        functools.partial(core_body, dp, expert),
        out_shape=(
            sds(cube, BF16),
            sds(cube, BF16),
            sds((part, width), F32),
            sds((part, width), F32),
            sds((dp, 2, width), F32),
        ),
        in_specs=[whole] * 10,
        out_specs=(whole,) * 5,
        scratch_shapes=scratch,
        compiler_params=pltpu.CompilerParams(
            collective_id=1, has_side_effects=True, vmem_limit_bytes=VMEM_BYTES
        ),
        name="core",
    )(
        xin,
        zin,
        cotangent,
        conv_weight,
        conv_bias[None, :],
        proj_weight,
        dt_weight,
        dt_bias[None, :],
        a_log,
        d_skip[None, :],
    )
    row = sds((1, width), F32)
    results = pl.pallas_call(
        functools.partial(output_body, 2 * states, taps),
        out_shape=(
            sds(cube, BF16),
            sds(cube, BF16),
            sds((part, width), F32),
            sds((2 * states, width), F32),
            sds((part, width), F32),
            sds((taps, width), F32),
            row,
            row,
            sds((states, width), F32),
            row,
        ),
        in_specs=[whole] * 5,
        out_specs=(whole,) * 10,
        compiler_params=pltpu.CompilerParams(vmem_limit_bytes=VMEM_BYTES),
        name="outputs",
    )(gate, gradx, proj, dtw, small)
    results = list(results)
    for i in (6, 7, 9):
        results[i] = results[i].reshape(width)
    return tuple(results)


def solution(mesh):
    return jax.shard_map(
        body,
        mesh=mesh,
        in_specs=(
            P(None, "dp", "expert"),
            P(None, "dp", "expert"),
            P(None, "dp", "expert"),
            P(None, "expert"),
            P("expert"),
            P("dp", "expert"),
            P("dp", "expert"),
            P("expert"),
            P(None, "expert"),
            P("expert"),
        ),
        out_specs=(
            P(None, "dp", "expert"),
            P(None, "dp", "expert"),
            P("dp", "expert"),
            P(None, "expert"),
            P("dp", "expert"),
            P(None, "expert"),
            P("expert"),
            P("expert"),
            P(None, "expert"),
            P("expert"),
        ),
        check_vma=False,
    )
```
